128 devices in a mesh: rep: 8 (over x_hi, y), fsdp: 16 (over z, x_lo, core).
Axes of the slice: x: 4 (x_hi: 2, x_lo: 2; x = x_hi * 2 + x_lo), y: 4, z: 4, core: 2. Of those that a mesh axis runs over, the one named last changes fastest.
Arguments:
- inner_weights: bfloat16 [8, 8192, 1024], P('rep', 'fsdp'), may hold values from -6 to 6
- master_weights: float32 [8, 8192, 1024], P('rep', 'fsdp'), may hold values from -6 to 6
- momentum: float32 [8, 8192, 1024], P('rep', 'fsdp'), may hold values from -6 to 6
- tokens: bfloat16 [8, 8192, 8192], P('rep', 'fsdp'), may hold values from -0.06591797 to 0.06591797
- partner: int32 [16, 8], P('fsdp'), may hold values from 0 to 7, as said below
Outputs:
- new_master: float32 [8, 8192, 1024], P('rep', 'fsdp')
- new_momentum: float32 [8, 8192, 1024], P('rep', 'fsdp')
- keys: bfloat16 [8, 8192, 1024], P('rep', 'fsdp')
The draws below stay inside these ranges and needn't reach their ends.
Inputs may be any that keep to these rules, and one draw needn't show every extreme that they name: For each block s, partner[s, r] = r XOR m_s for one mask m_s with 1 <= m_s < 8, the same m_s for all r, so each row of partner is an involution without fixed points.
All inputs are finite; a program needn't handle non-finite values.
Results may differ from the reference program's by a relative error of at most 0.005.
Values may be sent and summed in bfloat16 or wider, within the bound.
A program may use at most 128 MiB of HBM per device.

```python
import jax
import jax.numpy as jnp
from jax import lax

D = 8192
KV_WIDTH = 1024
N_REPLICA = 8
SHARDS = 16
TOKENS = 8192


def draw_partner(key, part):
    key = jax.random.fold_in(key, 7)
    block_masks = jax.random.randint(key, (SHARDS,), 1, N_REPLICA, dtype=jnp.int32)
    replica_ids = jnp.arange(N_REPLICA, dtype=jnp.int32)
    return jnp.bitwise_xor(replica_ids[None, :], block_masks[:, None])


def block_scale(stream_key, dims, split, least, top_value):
    def one(position, blocks):
        heights = jax.random.uniform(jax.random.fold_in(jax.random.fold_in(stream_key, 6), position), (blocks,), jnp.float32, least / len(split), top_value / len(split))
        return jnp.repeat(jnp.exp(heights), dims[position] // blocks).reshape((-1,) + (1,) * (len(dims) - position - 1))

    gain = one(*split[0])
    for cut in split[1:]:
        gain = gain * one(*cut)
    return gain


def bell_draw(stream_key, shape, width, most, pieces=(), kind=jnp.bfloat16):
    loudness = block_scale(stream_key, shape, pieces, -0.22, 0.18) if pieces else 1.0
    array = jax.random.normal(stream_key, shape, jnp.float32) * width * loudness
    return jnp.minimum(jnp.maximum(array, -most), most).astype(kind)


def setup_inputs(seed: int = 0) -> dict:
    streams_of = jax.random.split(jax.random.key(seed), 6)
    inner_weights = bell_draw(streams_of[0], (N_REPLICA, D, KV_WIDTH), 1.0, 6.0, ((0, 8), (1, 16)))
    master_weights = bell_draw(streams_of[1], (N_REPLICA, D, KV_WIDTH), 1.0, 6.0, ((0, 8), (1, 16)), jnp.float32)
    momentum = bell_draw(streams_of[2], (N_REPLICA, D, KV_WIDTH), 1.0, 6.0, ((0, 8), (1, 16)), jnp.float32)
    tokens = bell_draw(streams_of[3], (N_REPLICA, TOKENS, D), (D ** -0.5), 0.06591797, ((0, 8), (1, 16)))
    partner = draw_partner(jax.random.fold_in(streams_of[5], 71), 0)
    return dict(inner_weights=inner_weights, master_weights=master_weights, momentum=momentum, tokens=tokens, partner=partner)


def project_keys(pair):
    return jnp.dot(pair[0], pair[1], preferred_element_type=jnp.float32).astype(jnp.bfloat16)


def mate_blocks(values, partner):
    blocked = values.reshape(N_REPLICA, SHARDS, D // SHARDS, KV_WIDTH)
    index_table = jnp.transpose(partner).astype(jnp.int32)[:, :, None, None]
    picked = jnp.take_along_axis(blocked, index_table, axis=0)
    return picked.reshape(N_REPLICA, D, KV_WIDTH)


def reference(inner_weights, master_weights, momentum, tokens, partner):
    difference = master_weights - inner_weights.astype(jnp.float32)
    mean_difference = (difference + mate_blocks(difference, partner)) * 0.5
    mean_master = (master_weights + mate_blocks(master_weights, partner)) * 0.5
    new_momentum = 0.9 * momentum + mean_difference
    new_master = mean_master - 0.7 * (mean_difference + 0.9 * new_momentum)
    fresh = new_master.astype(jnp.bfloat16)
    keys = lax.map(project_keys, (tokens, fresh))
    return new_master, new_momentum, keys
```

```python
import functools

import jax
import jax.numpy as jnp
from jax import lax
from jax.experimental import pallas as pl
from jax.experimental.pallas import tpu as pltpu
from jax.sharding import PartitionSpec as P

MESH = pl.DeviceIdType.MESH
R, W = 64, 256
OFF_B, OFF_X, OFF_U, OFF_Z, OFF_F, OFF_D, OFF_M = 1, 2, 3, 4, 5, 6, 7


def kernel(
    part_ref, inner_ref, master_ref, mom_ref, tok_ref,
    out_master, out_mom, out_keys,
    m_v, mom_v, pay, buf_a, buf_b, buf_x, nm_v, nmom_v, fresh, tok_v, keys_v, acc,
    load_sem, send_sem, ra, rb, rx, rs, rz, rf, rd, out_sem,
):
    J = master_ref.shape[0]
    G = master_ref.shape[2] // W
    C = G * J
    slots_per_tick = 16 // J
    rows = J * R

    rep = lax.axis_index("rep")
    fs = lax.axis_index("fsdp")
    rep1 = rep + 1 - 2 * lax.rem(rep, 2)
    rep3 = rep + 3 - 2 * lax.rem(rep, 4)
    rep4 = lax.rem(rep + 4, 8)
    core = lax.rem(fs, 2)
    xlo = lax.rem(lax.div(fs, 2), 2)
    z = lax.div(fs, 4)
    sib = fs + 1 - 2 * core
    xn = fs + 2 - 4 * xlo
    zu = lax.rem(fs + 4, 16)
    zd = lax.rem(fs + 12, 16)

    dev_a, dev_b, dev_x = (rep1, fs), (rep3, fs), (rep4, fs)
    dev_s, dev_u, dev_d, dev_c = (rep, xn), (rep, zu), (rep, zd), (rep, sib)

    def load_mi(g):
        cols = pl.ds(g * W, W)
        return (
            pltpu.make_async_copy(master_ref.at[:, :, cols], m_v.at[pl.ds(g * J, J)], load_sem.at[0, g]),
            pltpu.make_async_copy(inner_ref.at[:, :, cols], pay.at[pl.ds(g * J, J), 1], load_sem.at[1, g]),
        )

    def load_mom(g):
        return pltpu.make_async_copy(mom_ref.at[:, :, pl.ds(g * W, W)], mom_v.at[pl.ds(g * J, J)], load_sem.at[2, g])

    load_tok = pltpu.make_async_copy(tok_ref, tok_v, load_sem.at[3, 0])
    for g in range(G):
        for c in load_mi(g):
            c.start()
    for g in range(G):
        load_mom(g).start()
    load_tok.start()

    barrier = pltpu.get_barrier_semaphore()
    for d in (dev_a, dev_b, dev_x, dev_s, dev_u, dev_d, dev_c):
        pl.semaphore_signal(barrier, inc=1, device_id=d, device_id_type=MESH)
    pl.semaphore_wait(barrier, 7)
    for g in range(G):
        for c in load_mi(g):
            c.wait()

    mask = jnp.bitwise_xor(part_ref[0, rep], rep)
    bit1 = lax.rem(lax.div(mask, 2), 2)
    pick_a = lax.rem(lax.rem(mask, 2) + bit1, 2) == 1
    pick_b = bit1 == 1
    pick_x = lax.div(mask, 4) == 1

    def remote(src, dst, k, recv, dev):
        return pltpu.make_async_remote_copy(
            src_ref=src, dst_ref=dst, send_sem=send_sem.at[k], recv_sem=recv, device_id=dev, device_id_type=MESH
        )

    def copy_a(t):
        return remote(pay.at[t], buf_a.at[t], 0, ra.at[t], dev_a)

    def copy_b(t):
        return remote(buf_a.at[t], buf_b.at[t], 1, rb.at[t], dev_b)

    def copy_x(t):
        return remote(buf_b.at[t], buf_x.at[t], 2, rx.at[t], dev_x)

    def copy_s(t):
        return remote(fresh.at[t, 0], fresh.at[t, 1], 3, rs.at[t], dev_s)

    def copy_up(t):
        return remote(fresh.at[t, pl.ds(0, 2)], fresh.at[t, pl.ds(6, 2)], 4, rz.at[0, t], dev_u)

    def copy_down(t):
        return remote(fresh.at[t, pl.ds(0, 2)], fresh.at[t, pl.ds(2, 2)], 5, rz.at[1, t], dev_d)

    def copy_fup(t):
        return remote(fresh.at[t, 6], fresh.at[t, 4], 6, rf.at[0, t], dev_u)

    def copy_fdown(t):
        return remote(fresh.at[t, 3], fresh.at[t, 5], 7, rf.at[1, t], dev_d)

    def copy_c(t):
        return remote(fresh.at[t, pl.ds(0, 8)], fresh.at[t, pl.ds(8, 8)], 8, rd.at[t], dev_c)

    def out_copies(g):
        cols = pl.ds(pl.multiple_of(g * W, W), W)
        span = pl.ds(g * J, J)
        return (
            pltpu.make_async_copy(nm_v.at[span], out_master.at[:, :, cols], out_sem.at[0, g]),
            pltpu.make_async_copy(nmom_v.at[span], out_mom.at[:, :, cols], out_sem.at[1, g]),
        )

    def out_key(g):
        cols = pl.ds(pl.multiple_of(g * W, W), W)
        return pltpu.make_async_copy(keys_v.at[g], out_keys.at[:, cols], out_sem.at[2, g])

    def tick(t, _):
        @pl.when(t < C)
        def _():
            pay[t, 0] = m_v[t].astype(jnp.bfloat16)
            copy_a(t).start()

        tb = t - OFF_B

        @pl.when((tb >= 0) & (tb < C))
        def _():
            copy_a(tb).wait_recv()
            buf_a[tb] = jnp.where(pick_a, buf_a[tb], pay[tb])
            copy_b(tb).start()

        tx = t - OFF_X

        @pl.when((tx >= 0) & (tx < C))
        def _():
            copy_b(tx).wait_recv()
            buf_b[tx] = jnp.where(pick_b, buf_b[tx], buf_a[tx])
            copy_x(tx).start()

        tu = t - OFF_U

        @pl.when(tu == 0)
        def _():
            for g in range(G):
                load_mom(g).wait()

        @pl.when((tu >= 0) & (tu < C))
        def _():
            copy_x(tu).wait_recv()
            their = jnp.where(pick_x, buf_x[tu], buf_b[tu])
            their_m = their[0].astype(jnp.float32)
            their_i = their[1].astype(jnp.float32)
            own_m = m_v[tu]
            own_i = pay[tu, 1].astype(jnp.float32)
            mean_d = ((own_m - own_i) + (their_m - their_i)) * 0.5
            mean_m = (own_m + their_m) * 0.5
            new_mom = 0.9 * mom_v[tu] + mean_d
            new_m = mean_m - 0.7 * (mean_d + 0.9 * new_mom)
            nmom_v[tu] = new_mom
            nm_v[tu] = new_m
            fresh[tu, 0] = new_m.astype(jnp.bfloat16)
            copy_s(tu).start()

        @pl.when((tu >= 0) & (tu < C) & (lax.rem(tu + C, J) == J - 1))
        def _():
            for c in out_copies(lax.div(tu, J)):
                c.start()

        tz = t - OFF_Z

        @pl.when((tz >= 0) & (tz < C))
        def _():
            copy_s(tz).wait_recv()
            copy_up(tz).start()
            copy_down(tz).start()

        tf = t - OFF_F

        @pl.when((tf >= 0) & (tf < C))
        def _():
            copy_up(tf).wait_recv()
            copy_fup(tf).start()
            copy_down(tf).wait_recv()
            copy_fdown(tf).start()

        td = t - OFF_D

        @pl.when((td >= 0) & (td < C))
        def _():
            copy_fup(td).wait_recv()
            copy_fdown(td).wait_recv()
            copy_c(td).start()

        tm = t - OFF_M

        @pl.when((tm >= 0) & (tm < C))
        def _():
            copy_c(tm).wait_recv()

        @pl.when(tm == J - 1)
        def _():
            load_tok.wait()

        u = tm - (J - 1)

        @pl.when(u >= 0)
        def _():
            g = lax.div(u, J)
            k = lax.rem(u, J)
            total = jnp.where(k == 0, 0.0, acc[...])
            for i in range(slots_per_tick):
                slot = k * slots_per_tick + i
                half = lax.div(slot, 8)
                low = lax.rem(slot, 8)
                oz = lax.rem(z + lax.div(low, 2), 4)
                ox = lax.rem(xlo + low, 2)
                oc = lax.rem(core + half, 2)
                owner = oz * 4 + ox * 2 + oc
                cols = pl.ds(pl.multiple_of(owner * rows, rows), rows)
                rhs = fresh[pl.ds(g * J, J), slot].reshape(rows, W)
                total += jnp.dot(tok_v[:, cols], rhs, preferred_element_type=jnp.float32)
            acc[...] = total

            @pl.when(k == J - 1)
            def _():
                keys_v[g] = total.astype(jnp.bfloat16)
                out_key(g).start()

        return 0

    lax.fori_loop(0, OFF_M + C + J - 1, tick, 0)

    everything = (
        (pay, buf_a, 0, ra.at[0], dev_a),
        (buf_a, buf_b, 1, rb.at[0], dev_b),
        (buf_b, buf_x, 2, rx.at[0], dev_x),
        (fresh.at[:, 0], fresh.at[:, 1], 3, rs.at[0], dev_s),
        (fresh.at[:, pl.ds(0, 2)], fresh.at[:, pl.ds(6, 2)], 4, rz.at[0, 0], dev_u),
        (fresh.at[:, pl.ds(0, 2)], fresh.at[:, pl.ds(2, 2)], 5, rz.at[1, 0], dev_d),
        (fresh.at[:, 6], fresh.at[:, 4], 6, rf.at[0, 0], dev_u),
        (fresh.at[:, 3], fresh.at[:, 5], 7, rf.at[1, 0], dev_d),
        (fresh.at[:, pl.ds(0, 8)], fresh.at[:, pl.ds(8, 8)], 8, rd.at[0], dev_c),
    )
    for src, dst, k, recv, dev in everything:
        remote(src, dst, k, recv, dev).wait_send()
    for g in range(G):
        for c in out_copies(g):
            c.wait()
        out_key(g).wait()


def local(inner_weights, master_weights, momentum, tokens, partner):
    rows, cols = master_weights.shape[1:]
    toks, depth = tokens.shape[1:]
    J, G = rows // R, cols // W
    C = G * J
    bf16, f32 = jnp.bfloat16, jnp.float32
    anyspace = pl.BlockSpec(memory_space=pl.ANY)
    dma = pltpu.SemaphoreType.DMA
    new_master, new_mom, keys = pl.pallas_call(
        kernel,
        out_shape=(
            jax.ShapeDtypeStruct((J, R, cols), f32),
            jax.ShapeDtypeStruct((J, R, cols), f32),
            jax.ShapeDtypeStruct((toks, cols), bf16),
        ),
        in_specs=[pl.BlockSpec(memory_space=pltpu.SMEM)] + [anyspace] * 4,
        out_specs=(anyspace,) * 3,
        scratch_shapes=[
            pltpu.VMEM((C, R, W), f32),
            pltpu.VMEM((C, R, W), f32),
            pltpu.VMEM((C, 2, R, W), bf16),
            pltpu.VMEM((C, 2, R, W), bf16),
            pltpu.VMEM((C, 2, R, W), bf16),
            pltpu.VMEM((C, 2, R, W), bf16),
            pltpu.VMEM((C, R, W), f32),
            pltpu.VMEM((C, R, W), f32),
            pltpu.VMEM((C, 16, R, W), bf16),
            pltpu.VMEM((toks, depth), bf16),
            pltpu.VMEM((G, toks, W), bf16),
            pltpu.VMEM((toks, W), f32),
            dma((4, G)),
            dma((9,)),
            dma((C,)),
            dma((C,)),
            dma((C,)),
            dma((C,)),
            dma((2, C)),
            dma((2, C)),
            dma((C,)),
            dma((3, G)),
        ],
        compiler_params=pltpu.CompilerParams(
            collective_id=0, has_side_effects=True, vmem_limit_bytes=60 * 1024 * 1024
        ),
        cost_estimate=pl.CostEstimate(
            flops=2 * toks * depth * cols, bytes_accessed=18 * 1024 * 1024, transcendentals=0
        ),
        name="gossip_keys",
    )(
        partner,
        inner_weights.reshape(J, R, cols),
        master_weights.reshape(J, R, cols),
        momentum.reshape(J, R, cols),
        tokens[0],
    )
    return (
        new_master.reshape(1, rows, cols),
        new_mom.reshape(1, rows, cols),
        keys[None],
    )


def solution(mesh):
    return jax.shard_map(
        local,
        mesh=mesh,
        in_specs=(
            P("rep", "fsdp", None),
            P("rep", "fsdp", None),
            P("rep", "fsdp", None),
            P("rep", "fsdp", None),
            P("fsdp", None),
        ),
        out_specs=(P("rep", "fsdp", None), P("rep", "fsdp", None), P("rep", "fsdp", None)),
        check_vma=False,
    )
```

```python
import functools

import jax
import jax.numpy as jnp
from jax import lax
from jax.experimental import pallas as pl
from jax.experimental.pallas import tpu as pltpu
from jax.sharding import PartitionSpec as P

MESH = pl.DeviceIdType.MESH
R, W = 64, 256
SUB = 128
OFF_B, OFF_X, OFF_U, OFF_Z, OFF_F, OFF_D, OFF_M = 2, 4, 6, 8, 10, 12, 14


def kernel(
    part_ref, inner_ref, master_ref, mom_ref, tok_ref,
    out_master, out_mom, out_keys,
    m_v, mom_v, pay, buf_a, buf_b, buf_x, nm_v, nmom_v, fresh, tok_v, keys_v, acc,
    load_sem, send_sem, ra, rb, rx, rs, rz, rf, rd, out_sem,
):
    J = master_ref.shape[0]
    G = master_ref.shape[2] // W
    C = G * J
    Q = SUB // R
    slots_per_tick = 16 // Q
    rows = J * R

    rep = lax.axis_index("rep")
    fs = lax.axis_index("fsdp")
    rep1 = rep + 1 - 2 * lax.rem(rep, 2)
    rep3 = rep + 3 - 2 * lax.rem(rep, 4)
    rep4 = lax.rem(rep + 4, 8)
    core = lax.rem(fs, 2)
    xlo = lax.rem(lax.div(fs, 2), 2)
    z = lax.div(fs, 4)
    sib = fs + 1 - 2 * core
    xn = fs + 2 - 4 * xlo
    zu = lax.rem(fs + 4, 16)
    zd = lax.rem(fs + 12, 16)

    dev_a, dev_b, dev_x = (rep1, fs), (rep3, fs), (rep4, fs)
    dev_s, dev_u, dev_d, dev_c = (rep, xn), (rep, zu), (rep, zd), (rep, sib)

    def load_mi(g):
        cols = pl.ds(g * W, W)
        return (
            pltpu.make_async_copy(master_ref.at[:, :, cols], m_v.at[pl.ds(g * J, J)], load_sem.at[0, g]),
            pltpu.make_async_copy(inner_ref.at[:, :, cols], pay.at[pl.ds(g * J, J), 1], load_sem.at[1, g]),
        )

    def load_mom(g):
        return pltpu.make_async_copy(mom_ref.at[:, :, pl.ds(g * W, W)], mom_v.at[pl.ds(g * J, J)], load_sem.at[2, g])

    load_tok = pltpu.make_async_copy(tok_ref, tok_v, load_sem.at[3, 0])
    for g in range(G):
        for c in load_mi(g):
            c.start()

    barrier = pltpu.get_barrier_semaphore()
    for d in (dev_a, dev_b, dev_x, dev_s, dev_u, dev_d, dev_c):
        pl.semaphore_signal(barrier, inc=1, device_id=d, device_id_type=MESH)
    pl.semaphore_wait(barrier, 7)
    for g in range(G):
        load_mom(g).start()
    load_tok.start()

    mask = jnp.bitwise_xor(part_ref[0, rep], rep)
    bit1 = lax.rem(lax.div(mask, 2), 2)
    pick_a = lax.rem(lax.rem(mask, 2) + bit1, 2) == 1
    pick_b = bit1 == 1
    pick_x = lax.div(mask, 4) == 1

    def remote(src, dst, k, recv, dev):
        return pltpu.make_async_remote_copy(
            src_ref=src, dst_ref=dst, send_sem=send_sem.at[k], recv_sem=recv, device_id=dev, device_id_type=MESH
        )

    def copy_a(t):
        return remote(pay.at[t], buf_a.at[t], 0, ra.at[t], dev_a)

    def copy_b(t):
        return remote(buf_a.at[t], buf_b.at[t], 1, rb.at[t], dev_b)

    def copy_x(t):
        return remote(buf_b.at[t], buf_x.at[t], 2, rx.at[t], dev_x)

    def copy_s(t):
        return remote(fresh.at[t, 0], fresh.at[t, 1], 3, rs.at[t], dev_s)

    def copy_up_one(t, slot):
        return remote(fresh.at[t, slot], fresh.at[t, 6 + slot], 4, rz.at[0, t], dev_u)

    def copy_down_one(t, slot):
        return remote(fresh.at[t, slot], fresh.at[t, 2 + slot], 5, rz.at[1, t], dev_d)

    def copy_up(t):
        return remote(fresh.at[t, pl.ds(0, 2)], fresh.at[t, pl.ds(6, 2)], 4, rz.at[0, t], dev_u)

    def copy_down(t):
        return remote(fresh.at[t, pl.ds(0, 2)], fresh.at[t, pl.ds(2, 2)], 5, rz.at[1, t], dev_d)

    def copy_fup(t):
        return remote(fresh.at[t, 6], fresh.at[t, 4], 6, rf.at[0, t], dev_u)

    def copy_fdown(t):
        return remote(fresh.at[t, 3], fresh.at[t, 5], 7, rf.at[1, t], dev_d)

    def copy_c(t):
        return remote(fresh.at[t, pl.ds(0, 8)], fresh.at[t, pl.ds(8, 8)], 8, rd.at[t], dev_c)

    def out_copies(g):
        cols = pl.ds(pl.multiple_of(g * W, W), W)
        span = pl.ds(g * J, J)
        return (
            pltpu.make_async_copy(nm_v.at[span], out_master.at[:, :, cols], out_sem.at[0, g]),
            pltpu.make_async_copy(nmom_v.at[span], out_mom.at[:, :, cols], out_sem.at[1, g]),
        )

    def out_key(g):
        cols = pl.ds(pl.multiple_of(g * W, W), W)
        return pltpu.make_async_copy(keys_v.at[g], out_keys.at[:, cols], out_sem.at[2, g])

    def tick(t, _):
        for g in range(G):
            @pl.when(t == g * J)
            def _():
                for c in load_mi(g):
                    c.wait()

        @pl.when(t < C)
        def _():
            pay[t, 0] = m_v[t].astype(jnp.bfloat16)
            copy_a(t).start()

        tb = t - OFF_B

        @pl.when((tb >= 0) & (tb < C))
        def _():
            copy_a(tb).wait_recv()
            buf_a[tb] = jnp.where(pick_a, buf_a[tb], pay[tb])
            copy_b(tb).start()

        tx = t - OFF_X

        @pl.when((tx >= 0) & (tx < C))
        def _():
            copy_b(tx).wait_recv()
            buf_b[tx] = jnp.where(pick_b, buf_b[tx], buf_a[tx])
            copy_x(tx).start()

        tu = t - OFF_U

        @pl.when(tu == 0)
        def _():
            for g in range(G):
                load_mom(g).wait()

        @pl.when((tu >= 0) & (tu < C))
        def _():
            copy_x(tu).wait_recv()
            their = jnp.where(pick_x, buf_x[tu], buf_b[tu])
            their_m = their[0].astype(jnp.float32)
            their_i = their[1].astype(jnp.float32)
            own_m = m_v[tu]
            own_i = pay[tu, 1].astype(jnp.float32)
            mean_d = ((own_m - own_i) + (their_m - their_i)) * 0.5
            mean_m = (own_m + their_m) * 0.5
            new_mom = 0.9 * mom_v[tu] + mean_d
            new_m = mean_m - 0.7 * (mean_d + 0.9 * new_mom)
            nmom_v[tu] = new_mom
            nm_v[tu] = new_m
            fresh[tu, 0] = new_m.astype(jnp.bfloat16)
            copy_s(tu).start()
            copy_up_one(tu, 0).start()
            copy_down_one(tu, 0).start()

        @pl.when((tu >= 0) & (tu < C) & (lax.rem(tu + C, J) == J - 1))
        def _():
            for c in out_copies(lax.div(tu, J)):
                c.start()

        tz = t - OFF_Z

        @pl.when((tz >= 0) & (tz < C))
        def _():
            copy_s(tz).wait_recv()
            copy_up_one(tz, 1).start()
            copy_down_one(tz, 1).start()

        tf = t - OFF_F

        @pl.when((tf >= 0) & (tf < C))
        def _():
            copy_up(tf).wait_recv()
            copy_fup(tf).start()
            copy_down(tf).wait_recv()
            copy_fdown(tf).start()

        td = t - OFF_D

        @pl.when((td >= 0) & (td < C))
        def _():
            copy_fup(td).wait_recv()
            copy_fdown(td).wait_recv()
            copy_c(td).start()

        tm = t - OFF_M

        @pl.when((tm >= 0) & (tm < C))
        def _():
            copy_c(tm).wait_recv()

        @pl.when(tm == Q - 1)
        def _():
            load_tok.wait()

        u = tm - (Q - 1)

        @pl.when(u >= 0)
        def _():
            q = lax.div(u, Q)
            k = lax.rem(u, Q)
            per_group = rows // SUB
            g = lax.div(q, per_group)
            part = lax.rem(q, per_group)
            first = (part == 0) & (k == 0)
            left, right = [], []
            for i in range(slots_per_tick):
                slot = k * slots_per_tick + i
                half = lax.div(slot, 8)
                low = lax.rem(slot, 8)
                oz = lax.rem(z + lax.div(low, 2), 4)
                ox = lax.rem(xlo + low, 2)
                oc = lax.rem(core + half, 2)
                owner = oz * 4 + ox * 2 + oc
                left.append(tok_v[:, pl.ds(pl.multiple_of(owner * rows + part * SUB, SUB), SUB)])
                right.append(fresh[pl.ds(q * Q, Q), slot].reshape(SUB, W))
            product = jnp.dot(
                jnp.concatenate(left, axis=1), jnp.concatenate(right, axis=0), preferred_element_type=jnp.float32
            )

            @pl.when(first)
            def _():
                acc[...] = product

            @pl.when(jnp.logical_not(first))
            def _():
                acc[...] += product

            @pl.when((part == per_group - 1) & (k == Q - 1))
            def _():
                keys_v[g] = acc[...].astype(jnp.bfloat16)
                out_key(g).start()

        return 0

    lax.fori_loop(0, OFF_M + C + Q - 1, tick, 0)

    everything = (
        (pay, buf_a, 0, ra.at[0], dev_a),
        (buf_a, buf_b, 1, rb.at[0], dev_b),
        (buf_b, buf_x, 2, rx.at[0], dev_x),
        (fresh.at[:, 0], fresh.at[:, 1], 3, rs.at[0], dev_s),
        (fresh.at[:, pl.ds(0, 2)], fresh.at[:, pl.ds(6, 2)], 4, rz.at[0, 0], dev_u),
        (fresh.at[:, pl.ds(0, 2)], fresh.at[:, pl.ds(2, 2)], 5, rz.at[1, 0], dev_d),
        (fresh.at[:, 6], fresh.at[:, 4], 6, rf.at[0, 0], dev_u),
        (fresh.at[:, 3], fresh.at[:, 5], 7, rf.at[1, 0], dev_d),
        (fresh.at[:, pl.ds(0, 8)], fresh.at[:, pl.ds(8, 8)], 8, rd.at[0], dev_c),
    )
    for src, dst, k, recv, dev in everything:
        remote(src, dst, k, recv, dev).wait_send()
    for g in range(G):
        for c in out_copies(g):
            c.wait()
        out_key(g).wait()


def local(inner_weights, master_weights, momentum, tokens, partner):
    rows, cols = master_weights.shape[1:]
    toks, depth = tokens.shape[1:]
    J, G = rows // R, cols // W
    C = G * J
    bf16, f32 = jnp.bfloat16, jnp.float32
    anyspace = pl.BlockSpec(memory_space=pl.ANY)
    dma = pltpu.SemaphoreType.DMA
    new_master, new_mom, keys = pl.pallas_call(
        kernel,
        out_shape=(
            jax.ShapeDtypeStruct((J, R, cols), f32),
            jax.ShapeDtypeStruct((J, R, cols), f32),
            jax.ShapeDtypeStruct((toks, cols), bf16),
        ),
        in_specs=[pl.BlockSpec(memory_space=pltpu.SMEM)] + [anyspace] * 4,
        out_specs=(anyspace,) * 3,
        scratch_shapes=[
            pltpu.VMEM((C, R, W), f32),
            pltpu.VMEM((C, R, W), f32),
            pltpu.VMEM((C, 2, R, W), bf16),
            pltpu.VMEM((C, 2, R, W), bf16),
            pltpu.VMEM((C, 2, R, W), bf16),
            pltpu.VMEM((C, 2, R, W), bf16),
            pltpu.VMEM((C, R, W), f32),
            pltpu.VMEM((C, R, W), f32),
            pltpu.VMEM((C, 16, R, W), bf16),
            pltpu.VMEM((toks, depth), bf16),
            pltpu.VMEM((G, toks, W), bf16),
            pltpu.VMEM((toks, W), f32),
            dma((4, G)),
            dma((9,)),
            dma((C,)),
            dma((C,)),
            dma((C,)),
            dma((C,)),
            dma((2, C)),
            dma((2, C)),
            dma((C,)),
            dma((3, G)),
        ],
        compiler_params=pltpu.CompilerParams(
            collective_id=0, has_side_effects=True, vmem_limit_bytes=60 * 1024 * 1024
        ),
        cost_estimate=pl.CostEstimate(
            flops=2 * toks * depth * cols, bytes_accessed=18 * 1024 * 1024, transcendentals=0
        ),
        name="gossip_keys",
    )(
        partner,
        inner_weights.reshape(J, R, cols),
        master_weights.reshape(J, R, cols),
        momentum.reshape(J, R, cols),
        tokens[0],
    )
    return (
        new_master.reshape(1, rows, cols),
        new_mom.reshape(1, rows, cols),
        keys[None],
    )


def solution(mesh):
    return jax.shard_map(
        local,
        mesh=mesh,
        in_specs=(
            P("rep", "fsdp", None),
            P("rep", "fsdp", None),
            P("rep", "fsdp", None),
            P("rep", "fsdp", None),
            P("fsdp", None),
        ),
        out_specs=(P("rep", "fsdp", None), P("rep", "fsdp", None), P("rep", "fsdp", None)),
        check_vma=False,
    )
```

```python
import functools

import jax
import jax.numpy as jnp
from jax import lax
from jax.experimental import pallas as pl
from jax.experimental.pallas import tpu as pltpu
from jax.sharding import PartitionSpec as P

MESH = pl.DeviceIdType.MESH
R, W = 64, 256
SUB = 128
OFF_B, OFF_X, OFF_U, OFF_Z, OFF_F, OFF_D, OFF_M = 2, 4, 6, 8, 10, 12, 14


def kernel(
    part_ref, inner_ref, master_ref, mom_ref, tok_ref,
    out_master, out_mom, out_keys,
    m_v, mom_v, pay, buf_a, buf_b, buf_x, nm_v, nmom_v, fresh, tok_v, keys_v, acc,
    part_s, part_sem, load_sem, send_sem, ra, rb, rx, rs, rz, rf, rd, out_sem,
):
    J = master_ref.shape[0]
    G = master_ref.shape[2] // W
    C = G * J
    Q = SUB // R
    slots_per_tick = 16 // Q
    rows = J * R

    rep = lax.axis_index("rep")
    fs = lax.axis_index("fsdp")
    rep1 = rep + 1 - 2 * lax.rem(rep, 2)
    rep3 = rep + 3 - 2 * lax.rem(rep, 4)
    rep4 = lax.rem(rep + 4, 8)
    core = lax.rem(fs, 2)
    xlo = lax.rem(lax.div(fs, 2), 2)
    z = lax.div(fs, 4)
    sib = fs + 1 - 2 * core
    xn = fs + 2 - 4 * xlo
    zu = lax.rem(fs + 4, 16)
    zd = lax.rem(fs + 12, 16)

    dev_a, dev_b, dev_x = (rep1, fs), (rep3, fs), (rep4, fs)
    dev_s, dev_u, dev_d, dev_c = (rep, xn), (rep, zu), (rep, zd), (rep, sib)

    def load_mi(g):
        cols = pl.ds(g * W, W)
        return (
            pltpu.make_async_copy(master_ref.at[:, :, cols], m_v.at[pl.ds(g * J, J)], load_sem.at[0, g]),
            pltpu.make_async_copy(inner_ref.at[:, :, cols], pay.at[pl.ds(g * J, J), 1], load_sem.at[1, g]),
        )

    def load_mom(g):
        return pltpu.make_async_copy(mom_ref.at[:, :, pl.ds(g * W, W)], mom_v.at[pl.ds(g * J, J)], load_sem.at[2, g])

    load_tok = pltpu.make_async_copy(tok_ref, tok_v, load_sem.at[3, 0])
    for c in load_mi(0):
        c.start()

    load_part = pltpu.make_async_copy(part_ref, part_s, part_sem)
    load_part.start()
    barrier = pltpu.get_barrier_semaphore()
    for d in (dev_a, dev_b, dev_x, dev_s, dev_u, dev_d, dev_c):
        pl.semaphore_signal(barrier, inc=1, device_id=d, device_id_type=MESH)
    pl.semaphore_wait(barrier, 7)
    for g in range(1, G):
        for c in load_mi(g):
            c.start()
    for g in range(G):
        load_mom(g).start()
    load_tok.start()

    load_part.wait()
    mask = jnp.bitwise_xor(part_s[0, rep], rep)
    bit1 = lax.rem(lax.div(mask, 2), 2)
    pick_a = lax.rem(lax.rem(mask, 2) + bit1, 2) == 1
    pick_b = bit1 == 1
    pick_x = lax.div(mask, 4) == 1

    def remote(src, dst, k, recv, dev):
        return pltpu.make_async_remote_copy(
            src_ref=src, dst_ref=dst, send_sem=send_sem.at[k], recv_sem=recv, device_id=dev, device_id_type=MESH
        )

    def copy_a(t):
        return remote(pay.at[t], buf_a.at[t], 0, ra.at[t], dev_a)

    def copy_b(t):
        return remote(buf_a.at[t], buf_b.at[t], 1, rb.at[t], dev_b)

    def copy_x(t):
        return remote(buf_b.at[t], buf_x.at[t], 2, rx.at[t], dev_x)

    def copy_s(t):
        return remote(fresh.at[t, 0], fresh.at[t, 1], 3, rs.at[t], dev_s)

    def copy_up_one(t, slot):
        return remote(fresh.at[t, slot], fresh.at[t, 6 + slot], 4, rz.at[0, t], dev_u)

    def copy_down_one(t, slot):
        return remote(fresh.at[t, slot], fresh.at[t, 2 + slot], 5, rz.at[1, t], dev_d)

    def copy_up(t):
        return remote(fresh.at[t, pl.ds(0, 2)], fresh.at[t, pl.ds(6, 2)], 4, rz.at[0, t], dev_u)

    def copy_down(t):
        return remote(fresh.at[t, pl.ds(0, 2)], fresh.at[t, pl.ds(2, 2)], 5, rz.at[1, t], dev_d)

    def copy_fup(t):
        return remote(fresh.at[t, 6], fresh.at[t, 4], 6, rf.at[0, t], dev_u)

    def copy_fdown(t):
        return remote(fresh.at[t, 3], fresh.at[t, 5], 7, rf.at[1, t], dev_d)

    def copy_c(t):
        return remote(fresh.at[t, pl.ds(0, 8)], fresh.at[t, pl.ds(8, 8)], 8, rd.at[t], dev_c)

    def out_copies(g):
        cols = pl.ds(pl.multiple_of(g * W, W), W)
        span = pl.ds(g * J, J)
        return (
            pltpu.make_async_copy(nm_v.at[span], out_master.at[:, :, cols], out_sem.at[0, g]),
            pltpu.make_async_copy(nmom_v.at[span], out_mom.at[:, :, cols], out_sem.at[1, g]),
        )

    def out_key(g):
        cols = pl.ds(pl.multiple_of(g * W, W), W)
        return pltpu.make_async_copy(keys_v.at[g], out_keys.at[:, cols], out_sem.at[2, g])

    def tick(t, _):
        for g in range(G):
            @pl.when(t == g * J)
            def _():
                for c in load_mi(g):
                    c.wait()

        @pl.when(t < C)
        def _():
            pay[t, 0] = m_v[t].astype(jnp.bfloat16)
            copy_a(t).start()

        tb = t - OFF_B

        @pl.when((tb >= 0) & (tb < C))
        def _():
            copy_a(tb).wait_recv()
            buf_a[tb] = jnp.where(pick_a, buf_a[tb], pay[tb])
            copy_b(tb).start()

        tx = t - OFF_X

        @pl.when((tx >= 0) & (tx < C))
        def _():
            copy_b(tx).wait_recv()
            buf_b[tx] = jnp.where(pick_b, buf_b[tx], buf_a[tx])
            copy_x(tx).start()

        tu = t - OFF_U

        @pl.when(tu == 0)
        def _():
            for g in range(G):
                load_mom(g).wait()

        @pl.when((tu >= 0) & (tu < C))
        def _():
            copy_x(tu).wait_recv()
            their = jnp.where(pick_x, buf_x[tu], buf_b[tu])
            their_m = their[0].astype(jnp.float32)
            their_i = their[1].astype(jnp.float32)
            own_m = m_v[tu]
            own_i = pay[tu, 1].astype(jnp.float32)
            mean_d = ((own_m - own_i) + (their_m - their_i)) * 0.5
            mean_m = (own_m + their_m) * 0.5
            new_mom = 0.9 * mom_v[tu] + mean_d
            new_m = mean_m - 0.7 * (mean_d + 0.9 * new_mom)
            nmom_v[tu] = new_mom
            nm_v[tu] = new_m
            fresh[tu, 0] = new_m.astype(jnp.bfloat16)
            copy_s(tu).start()
            copy_up_one(tu, 0).start()
            copy_down_one(tu, 0).start()

        @pl.when((tu >= 0) & (tu < C) & (lax.rem(tu + C, J) == J - 1))
        def _():
            for c in out_copies(lax.div(tu, J)):
                c.start()

        tz = t - OFF_Z

        @pl.when((tz >= 0) & (tz < C))
        def _():
            copy_s(tz).wait_recv()
            copy_up_one(tz, 1).start()
            copy_down_one(tz, 1).start()

        tf = t - OFF_F

        @pl.when((tf >= 0) & (tf < C))
        def _():
            copy_up(tf).wait_recv()
            copy_fup(tf).start()
            copy_down(tf).wait_recv()
            copy_fdown(tf).start()

        td = t - OFF_D

        @pl.when((td >= 0) & (td < C))
        def _():
            copy_fup(td).wait_recv()
            copy_fdown(td).wait_recv()
            copy_c(td).start()

        tm = t - OFF_M

        @pl.when((tm >= 0) & (tm < C))
        def _():
            copy_c(tm).wait_recv()

        @pl.when(tm == Q - 1)
        def _():
            load_tok.wait()

        u = tm - (Q - 1)

        @pl.when(u >= 0)
        def _():
            q = lax.div(u, Q)
            k = lax.rem(u, Q)
            per_group = rows // SUB
            g = lax.div(q, per_group)
            part = lax.rem(q, per_group)
            first = (part == 0) & (k == 0)
            left, right = [], []
            for i in range(slots_per_tick):
                slot = k * slots_per_tick + i
                half = lax.div(slot, 8)
                low = lax.rem(slot, 8)
                oz = lax.rem(z + lax.div(low, 2), 4)
                ox = lax.rem(xlo + low, 2)
                oc = lax.rem(core + half, 2)
                owner = oz * 4 + ox * 2 + oc
                left.append(tok_v[:, pl.ds(pl.multiple_of(owner * rows + part * SUB, SUB), SUB)])
                right.append(fresh[pl.ds(q * Q, Q), slot].reshape(SUB, W))
            product = jnp.dot(
                jnp.concatenate(left, axis=1), jnp.concatenate(right, axis=0), preferred_element_type=jnp.float32
            )

            @pl.when(first)
            def _():
                acc[...] = product

            @pl.when(jnp.logical_not(first))
            def _():
                acc[...] += product

            @pl.when((part == per_group - 1) & (k == Q - 1))
            def _():
                keys_v[g] = acc[...].astype(jnp.bfloat16)
                out_key(g).start()

        return 0

    lax.fori_loop(0, OFF_M + C + Q - 1, tick, 0)

    everything = (
        (pay, buf_a, 0, ra.at[0], dev_a),
        (buf_a, buf_b, 1, rb.at[0], dev_b),
        (buf_b, buf_x, 2, rx.at[0], dev_x),
        (fresh.at[:, 0], fresh.at[:, 1], 3, rs.at[0], dev_s),
        (fresh.at[:, pl.ds(0, 2)], fresh.at[:, pl.ds(6, 2)], 4, rz.at[0, 0], dev_u),
        (fresh.at[:, pl.ds(0, 2)], fresh.at[:, pl.ds(2, 2)], 5, rz.at[1, 0], dev_d),
        (fresh.at[:, 6], fresh.at[:, 4], 6, rf.at[0, 0], dev_u),
        (fresh.at[:, 3], fresh.at[:, 5], 7, rf.at[1, 0], dev_d),
        (fresh.at[:, pl.ds(0, 8)], fresh.at[:, pl.ds(8, 8)], 8, rd.at[0], dev_c),
    )
    for src, dst, k, recv, dev in everything:
        remote(src, dst, k, recv, dev).wait_send()
    for g in range(G):
        for c in out_copies(g):
            c.wait()
        out_key(g).wait()


def local(inner_weights, master_weights, momentum, tokens, partner):
    rows, cols = master_weights.shape[1:]
    toks, depth = tokens.shape[1:]
    J, G = rows // R, cols // W
    C = G * J
    bf16, f32 = jnp.bfloat16, jnp.float32
    anyspace = pl.BlockSpec(memory_space=pl.ANY)
    dma = pltpu.SemaphoreType.DMA
    new_master, new_mom, keys = pl.pallas_call(
        kernel,
        out_shape=(
            jax.ShapeDtypeStruct((J, R, cols), f32),
            jax.ShapeDtypeStruct((J, R, cols), f32),
            jax.ShapeDtypeStruct((toks, cols), bf16),
        ),
        in_specs=[pl.BlockSpec(memory_space=pltpu.HBM)] * 5,
        out_specs=(anyspace,) * 3,
        scratch_shapes=[
            pltpu.VMEM((C, R, W), f32),
            pltpu.VMEM((C, R, W), f32),
            pltpu.VMEM((C, 2, R, W), bf16),
            pltpu.VMEM((C, 2, R, W), bf16),
            pltpu.VMEM((C, 2, R, W), bf16),
            pltpu.VMEM((C, 2, R, W), bf16),
            pltpu.VMEM((C, R, W), f32),
            pltpu.VMEM((C, R, W), f32),
            pltpu.VMEM((C, 16, R, W), bf16),
            pltpu.VMEM((toks, depth), bf16),
            pltpu.VMEM((G, toks, W), bf16),
            pltpu.VMEM((toks, W), f32),
            pltpu.SMEM((1, 8), jnp.int32),
            dma,
            dma((4, G)),
            dma((9,)),
            dma((C,)),
            dma((C,)),
            dma((C,)),
            dma((C,)),
            dma((2, C)),
            dma((2, C)),
            dma((C,)),
            dma((3, G)),
        ],
        compiler_params=pltpu.CompilerParams(
            collective_id=0, has_side_effects=True, vmem_limit_bytes=47104 * 1024
        ),
        cost_estimate=pl.CostEstimate(
            flops=2 * toks * depth * cols, bytes_accessed=18 * 1024 * 1024, transcendentals=0
        ),
        name="gossip_keys",
    )(
        partner,
        inner_weights.reshape(J, R, cols),
        master_weights.reshape(J, R, cols),
        momentum.reshape(J, R, cols),
        tokens[0],
    )
    return (
        new_master.reshape(1, rows, cols),
        new_mom.reshape(1, rows, cols),
        keys[None],
    )


def solution(mesh):
    return jax.shard_map(
        local,
        mesh=mesh,
        in_specs=(
            P("rep", "fsdp", None),
            P("rep", "fsdp", None),
            P("rep", "fsdp", None),
            P("rep", "fsdp", None),
            P("fsdp", None),
        ),
        out_specs=(P("rep", "fsdp", None), P("rep", "fsdp", None), P("rep", "fsdp", None)),
        check_vma=False,
    )
```

```python
import functools

import jax
import jax.numpy as jnp
from jax import lax
from jax.experimental import pallas as pl
from jax.experimental.pallas import tpu as pltpu
from jax.sharding import PartitionSpec as P

MESH = pl.DeviceIdType.MESH
R, W = 64, 256
SUB = 128
OFF_2, OFF_3, OFF_U, OFF_Z, OFF_F, OFF_D, OFF_M = 3, 5, 7, 9, 11, 13, 15
LATE = 2
EARLY = OFF_Z - OFF_U


def kernel(
    part_ref, inner_ref, master_ref, mom_ref, tok_ref,
    out_master, out_mom, out_keys,
    m_v, mom_v, pay, buf_1, buf_2, buf_3, nm_v, nmom_v, fresh, tok_v, keys_v, acc,
    part_s, part_sem, load_sem, send_sem, r1, r2, r3, rs, rz, rf, rd, out_sem,
):
    J = master_ref.shape[0]
    G = master_ref.shape[2] // W
    C = G * J
    Q = SUB // R
    slots_per_tick = 16 // Q
    rows = J * R

    rep = lax.axis_index("rep")
    fs = lax.axis_index("fsdp")
    rep1 = rep + 1 - 2 * lax.rem(rep, 2)
    rep3 = rep + 3 - 2 * lax.rem(rep, 4)
    rep4 = lax.rem(rep + 4, 8)
    core = lax.rem(fs, 2)
    xlo = lax.rem(lax.div(fs, 2), 2)
    z = lax.div(fs, 4)
    sib = fs + 1 - 2 * core
    xn = fs + 2 - 4 * xlo
    zu = lax.rem(fs + 4, 16)
    zd = lax.rem(fs + 12, 16)

    dev_x, dev_a, dev_b = (rep4, fs), (rep1, fs), (rep3, fs)
    dev_s, dev_u, dev_d, dev_c = (rep, xn), (rep, zu), (rep, zd), (rep, sib)
    dev_xu, dev_xd = (rep, lax.rem(xn + 4, 16)), (rep, lax.rem(xn + 12, 16))

    def load_mi(g):
        cols = pl.ds(g * W, W)
        return (
            pltpu.make_async_copy(master_ref.at[:, :, cols], m_v.at[pl.ds(g * J, J)], load_sem.at[0, g]),
            pltpu.make_async_copy(inner_ref.at[:, :, cols], pay.at[pl.ds(g * J, J), 1], load_sem.at[1, g]),
        )

    def load_mom(g):
        return pltpu.make_async_copy(mom_ref.at[:, :, pl.ds(g * W, W)], mom_v.at[pl.ds(g * J, J)], load_sem.at[2, g])

    load_tok = pltpu.make_async_copy(tok_ref, tok_v, load_sem.at[3, 0])
    for c in load_mi(0):
        c.start()

    load_part = pltpu.make_async_copy(part_ref, part_s, part_sem)
    load_part.start()
    barrier = pltpu.get_barrier_semaphore()
    for d in (dev_a, dev_b, dev_x, dev_s, dev_u, dev_d, dev_c, dev_xu, dev_xd):
        pl.semaphore_signal(barrier, inc=1, device_id=d, device_id_type=MESH)
    pl.semaphore_wait(barrier, 9)
    for g in range(1, G):
        for c in load_mi(g):
            c.start()
    for g in range(G):
        load_mom(g).start()
    load_tok.start()

    load_part.wait()
    mask = jnp.bitwise_xor(part_s[0, rep], rep)
    bit1 = lax.rem(lax.div(mask, 2), 2)
    pick_a = lax.rem(lax.rem(mask, 2) + bit1, 2) == 1
    pick_b = bit1 == 1
    pick_x = lax.div(mask, 4) == 1

    def remote(src, dst, k, recv, dev):
        return pltpu.make_async_remote_copy(
            src_ref=src, dst_ref=dst, send_sem=send_sem.at[k], recv_sem=recv, device_id=dev, device_id_type=MESH
        )

    def copy_1(t):
        return remote(pay.at[t], buf_1.at[t], 0, r1.at[t], dev_x)

    def copy_2(t):
        return remote(buf_1.at[t], buf_2.at[t], 1, r2.at[t], dev_a)

    def copy_3(t):
        return remote(buf_2.at[t], buf_3.at[t], 2, r3.at[t], dev_b)

    def copy_s(t):
        return remote(fresh.at[t, 0], fresh.at[t, 1], 3, rs.at[t], dev_s)

    def copy_up_one(t, slot):
        return remote(fresh.at[t, slot], fresh.at[t, 6 + slot], 4 + 7 * slot, rz.at[0, t], dev_u)

    def copy_down_one(t, slot):
        return remote(fresh.at[t, slot], fresh.at[t, 2 + slot], 5 + 7 * slot, rz.at[1, t], dev_d)

    def copy_xup(t):
        return remote(fresh.at[t, 0], fresh.at[t, 7], 9, rz.at[0, t], dev_xu)

    def copy_xdown(t):
        return remote(fresh.at[t, 0], fresh.at[t, 3], 10, rz.at[1, t], dev_xd)

    def copy_up(t):
        return remote(fresh.at[t, pl.ds(0, 2)], fresh.at[t, pl.ds(6, 2)], 4, rz.at[0, t], dev_u)

    def copy_down(t):
        return remote(fresh.at[t, pl.ds(0, 2)], fresh.at[t, pl.ds(2, 2)], 5, rz.at[1, t], dev_d)

    def copy_fup(t):
        return remote(fresh.at[t, 6], fresh.at[t, 4], 6, rf.at[0, t], dev_u)

    def copy_fdown(t):
        return remote(fresh.at[t, 3], fresh.at[t, 5], 7, rf.at[1, t], dev_d)

    def copy_c(t):
        return remote(fresh.at[t, pl.ds(0, 8)], fresh.at[t, pl.ds(8, 8)], 8, rd.at[t], dev_c)

    def out_copies(g):
        cols = pl.ds(pl.multiple_of(g * W, W), W)
        span = pl.ds(g * J, J)
        return (
            pltpu.make_async_copy(nm_v.at[span], out_master.at[:, :, cols], out_sem.at[0, g]),
            pltpu.make_async_copy(nmom_v.at[span], out_mom.at[:, :, cols], out_sem.at[1, g]),
        )

    def out_key(g):
        cols = pl.ds(pl.multiple_of(g * W, W), W)
        return pltpu.make_async_copy(keys_v.at[g], out_keys.at[:, cols], out_sem.at[2, g])

    def forward(t):
        copy_up(t).wait_recv()
        copy_fup(t).start()
        copy_down(t).wait_recv()
        copy_fdown(t).start()

    def to_sibling(t):
        copy_fup(t).wait_recv()
        copy_fdown(t).wait_recv()
        copy_c(t).start()

    def tick(t, _):
        for g in range(G):
            @pl.when(t == g * J)
            def _():
                for c in load_mi(g):
                    c.wait()

        @pl.when(t < C)
        def _():
            pay[t, 0] = m_v[t].astype(jnp.bfloat16)
            copy_1(t).start()

        t2 = t - OFF_2

        @pl.when((t2 >= 0) & (t2 < C))
        def _():
            copy_1(t2).wait_recv()
            buf_1[t2] = jnp.where(pick_x, buf_1[t2], pay[t2])
            copy_2(t2).start()

        t3 = t - OFF_3

        @pl.when((t3 >= 0) & (t3 < C))
        def _():
            copy_2(t3).wait_recv()
            buf_2[t3] = jnp.where(pick_a, buf_2[t3], buf_1[t3])
            copy_3(t3).start()

        tu = t - OFF_U

        @pl.when(tu == 0)
        def _():
            for g in range(G):
                load_mom(g).wait()

        @pl.when((tu >= 0) & (tu < C))
        def _():
            copy_3(tu).wait_recv()
            their = jnp.where(pick_b, buf_3[tu], buf_2[tu])
            their_m = their[0].astype(jnp.float32)
            their_i = their[1].astype(jnp.float32)
            own_m = m_v[tu]
            own_i = pay[tu, 1].astype(jnp.float32)
            mean_d = ((own_m - own_i) + (their_m - their_i)) * 0.5
            mean_m = (own_m + their_m) * 0.5
            new_mom = 0.9 * mom_v[tu] + mean_d
            new_m = mean_m - 0.7 * (mean_d + 0.9 * new_mom)
            nmom_v[tu] = new_mom
            nm_v[tu] = new_m
            fresh[tu, 0] = new_m.astype(jnp.bfloat16)
            copy_s(tu).start()
            copy_up_one(tu, 0).start()
            copy_down_one(tu, 0).start()

            @pl.when(tu >= C - LATE)
            def _():
                copy_xup(tu).start()
                copy_xdown(tu).start()

        @pl.when((tu >= 0) & (tu < C) & (lax.rem(tu + C, J) == J - 1))
        def _():
            for c in out_copies(lax.div(tu, J)):
                c.start()

        tz = t - OFF_Z

        @pl.when((tz >= 0) & (tz < C))
        def _():
            copy_s(tz).wait_recv()

            @pl.when(tz < C - LATE)
            def _():
                copy_up_one(tz, 1).start()
                copy_down_one(tz, 1).start()

        tf = t - OFF_F
        tl = tf + EARLY

        @pl.when((tf >= 0) & (tf < C - LATE))
        def _():
            forward(tf)

        @pl.when((tl >= C - LATE) & (tl < C))
        def _():
            forward(tl)

        td = t - OFF_D
        te = td + EARLY

        @pl.when((td >= 0) & (td < C - LATE))
        def _():
            to_sibling(td)

        @pl.when((te >= C - LATE) & (te < C))
        def _():
            to_sibling(te)

        tm = t - OFF_M

        @pl.when((tm >= 0) & (tm < C))
        def _():
            copy_c(tm).wait_recv()

        @pl.when(tm == Q - 1)
        def _():
            load_tok.wait()

        u = tm - (Q - 1)

        @pl.when(u >= 0)
        def _():
            q = lax.div(u, Q)
            k = lax.rem(u, Q)
            per_group = rows // SUB
            g = lax.div(q, per_group)
            part = lax.rem(q, per_group)
            first = (part == 0) & (k == 0)
            left, right = [], []
            for i in range(slots_per_tick):
                slot = k * slots_per_tick + i
                half = lax.div(slot, 8)
                low = lax.rem(slot, 8)
                oz = lax.rem(z + lax.div(low, 2), 4)
                ox = lax.rem(xlo + low, 2)
                oc = lax.rem(core + half, 2)
                owner = oz * 4 + ox * 2 + oc
                left.append(tok_v[:, pl.ds(pl.multiple_of(owner * rows + part * SUB, SUB), SUB)])
                right.append(fresh[pl.ds(q * Q, Q), slot].reshape(SUB, W))
            product = jnp.dot(
                jnp.concatenate(left, axis=1), jnp.concatenate(right, axis=0), preferred_element_type=jnp.float32
            )

            @pl.when(first)
            def _():
                acc[...] = product

            @pl.when(jnp.logical_not(first))
            def _():
                acc[...] += product

            @pl.when((part == per_group - 1) & (k == Q - 1))
            def _():
                keys_v[g] = acc[...].astype(jnp.bfloat16)
                out_key(g).start()

        return 0

    lax.fori_loop(0, OFF_M + C + Q - 1, tick, 0)

    early, last = pl.ds(0, C - LATE), pl.ds(C - LATE, LATE)
    everything = (
        (pay, buf_1, 0, r1.at[0], dev_x),
        (buf_1, buf_2, 1, r2.at[0], dev_a),
        (buf_2, buf_3, 2, r3.at[0], dev_b),
        (fresh.at[:, 0], fresh.at[:, 1], 3, rs.at[0], dev_s),
        (fresh.at[:, 0], fresh.at[:, 6], 4, rz.at[0, 0], dev_u),
        (fresh.at[:, 0], fresh.at[:, 2], 5, rz.at[1, 0], dev_d),
        (fresh.at[early, 1], fresh.at[early, 7], 11, rz.at[0, 0], dev_u),
        (fresh.at[early, 1], fresh.at[early, 3], 12, rz.at[1, 0], dev_d),
        (fresh.at[last, 0], fresh.at[last, 7], 9, rz.at[0, 0], dev_xu),
        (fresh.at[last, 0], fresh.at[last, 3], 10, rz.at[1, 0], dev_xd),
        (fresh.at[:, 6], fresh.at[:, 4], 6, rf.at[0, 0], dev_u),
        (fresh.at[:, 3], fresh.at[:, 5], 7, rf.at[1, 0], dev_d),
        (fresh.at[:, pl.ds(0, 8)], fresh.at[:, pl.ds(8, 8)], 8, rd.at[0], dev_c),
    )
    for src, dst, k, recv, dev in everything:
        remote(src, dst, k, recv, dev).wait_send()
    for g in range(G):
        for c in out_copies(g):
            c.wait()
        out_key(g).wait()


def local(inner_weights, master_weights, momentum, tokens, partner):
    rows, cols = master_weights.shape[1:]
    toks, depth = tokens.shape[1:]
    J, G = rows // R, cols // W
    C = G * J
    bf16, f32 = jnp.bfloat16, jnp.float32
    anyspace = pl.BlockSpec(memory_space=pl.ANY)
    dma = pltpu.SemaphoreType.DMA
    new_master, new_mom, keys = pl.pallas_call(
        kernel,
        out_shape=(
            jax.ShapeDtypeStruct((J, R, cols), f32),
            jax.ShapeDtypeStruct((J, R, cols), f32),
            jax.ShapeDtypeStruct((toks, cols), bf16),
        ),
        in_specs=[pl.BlockSpec(memory_space=pltpu.HBM)] * 5,
        out_specs=(anyspace,) * 3,
        scratch_shapes=[
            pltpu.VMEM((C, R, W), f32),
            pltpu.VMEM((C, R, W), f32),
            pltpu.VMEM((C, 2, R, W), bf16),
            pltpu.VMEM((C, 2, R, W), bf16),
            pltpu.VMEM((C, 2, R, W), bf16),
            pltpu.VMEM((C, 2, R, W), bf16),
            pltpu.VMEM((C, R, W), f32),
            pltpu.VMEM((C, R, W), f32),
            pltpu.VMEM((C, 16, R, W), bf16),
            pltpu.VMEM((toks, depth), bf16),
            pltpu.VMEM((G, toks, W), bf16),
            pltpu.VMEM((toks, W), f32),
            pltpu.SMEM((1, 8), jnp.int32),
            dma,
            dma((4, G)),
            dma((13,)),
            dma((C,)),
            dma((C,)),
            dma((C,)),
            dma((C,)),
            dma((2, C)),
            dma((2, C)),
            dma((C,)),
            dma((3, G)),
        ],
        compiler_params=pltpu.CompilerParams(
            collective_id=0, has_side_effects=True, vmem_limit_bytes=47104 * 1024
        ),
        cost_estimate=pl.CostEstimate(
            flops=2 * toks * depth * cols, bytes_accessed=18 * 1024 * 1024, transcendentals=0
        ),
        name="gossip_keys",
    )(
        partner,
        inner_weights.reshape(J, R, cols),
        master_weights.reshape(J, R, cols),
        momentum.reshape(J, R, cols),
        tokens[0],
    )
    return (
        new_master.reshape(1, rows, cols),
        new_mom.reshape(1, rows, cols),
        keys[None],
    )


def solution(mesh):
    return jax.shard_map(
        local,
        mesh=mesh,
        in_specs=(
            P("rep", "fsdp", None),
            P("rep", "fsdp", None),
            P("rep", "fsdp", None),
            P("rep", "fsdp", None),
            P("fsdp", None),
        ),
        out_specs=(P("rep", "fsdp", None), P("rep", "fsdp", None), P("rep", "fsdp", None)),
        check_vma=False,
    )
```

```python
import functools

import jax
import jax.numpy as jnp
from jax import lax
from jax.experimental import pallas as pl
from jax.experimental.pallas import tpu as pltpu
from jax.sharding import PartitionSpec as P

MESH = pl.DeviceIdType.MESH
R, W = 64, 256
SUB = 128
OFF_2, OFF_3, OFF_U, OFF_Z, OFF_F, OFF_D, OFF_M = 3, 5, 7, 9, 11, 13, 15
LATE = 2
SHARES = 3
EARLY = OFF_Z - OFF_U


def kernel(
    part_ref, inner_ref, master_ref, mom_ref, tok_ref,
    out_master, out_mom, out_keys,
    m_v, mom_v, pay, buf_1, buf_2, buf_3, nm_v, nmom_v, fresh, tok_v, keys_v, acc,
    part_s, part_sem, load_sem, send_sem, r1, r2, r3, rs, rz, rf, rq, rd, out_sem,
):
    J = master_ref.shape[0]
    G = master_ref.shape[2] // W
    C = G * J
    Q = SUB // R
    slots_per_tick = 16 // Q
    rows = J * R

    rep = lax.axis_index("rep")
    fs = lax.axis_index("fsdp")
    rep1 = rep + 1 - 2 * lax.rem(rep, 2)
    rep3 = rep + 3 - 2 * lax.rem(rep, 4)
    rep4 = lax.rem(rep + 4, 8)
    core = lax.rem(fs, 2)
    xlo = lax.rem(lax.div(fs, 2), 2)
    z = lax.div(fs, 4)
    sib = fs + 1 - 2 * core
    xn = fs + 2 - 4 * xlo
    zu = lax.rem(fs + 4, 16)
    zd = lax.rem(fs + 12, 16)

    dev_x, dev_a, dev_b = (rep4, fs), (rep1, fs), (rep3, fs)
    dev_s, dev_u, dev_d, dev_c = (rep, xn), (rep, zu), (rep, zd), (rep, sib)
    dev_xu, dev_xd = (rep, lax.rem(xn + 4, 16)), (rep, lax.rem(xn + 12, 16))

    def load_mi(g):
        cols = pl.ds(g * W, W)
        return (
            pltpu.make_async_copy(master_ref.at[:, :, cols], m_v.at[pl.ds(g * J, J)], load_sem.at[0, g]),
            pltpu.make_async_copy(inner_ref.at[:, :, cols], pay.at[pl.ds(g * J, J), 1], load_sem.at[1, g]),
        )

    def load_mom(g):
        return pltpu.make_async_copy(mom_ref.at[:, :, pl.ds(g * W, W)], mom_v.at[pl.ds(g * J, J)], load_sem.at[2, g])

    load_tok = pltpu.make_async_copy(tok_ref, tok_v, load_sem.at[3, 0])
    for c in load_mi(0):
        c.start()

    load_part = pltpu.make_async_copy(part_ref, part_s, part_sem)
    load_part.start()
    barrier = pltpu.get_barrier_semaphore()
    for d in (dev_a, dev_b, dev_x, dev_s, dev_u, dev_d, dev_c, dev_xu, dev_xd):
        pl.semaphore_signal(barrier, inc=1, device_id=d, device_id_type=MESH)
    pl.semaphore_wait(barrier, 9)
    for g in range(1, G):
        for c in load_mi(g):
            c.start()
    for g in range(G):
        load_mom(g).start()
    load_tok.start()

    load_part.wait()
    mask = jnp.bitwise_xor(part_s[0, rep], rep)
    bit1 = lax.rem(lax.div(mask, 2), 2)
    pick_a = lax.rem(lax.rem(mask, 2) + bit1, 2) == 1
    pick_b = bit1 == 1
    pick_x = lax.div(mask, 4) == 1

    def remote(src, dst, k, recv, dev):
        return pltpu.make_async_remote_copy(
            src_ref=src, dst_ref=dst, send_sem=send_sem.at[k], recv_sem=recv, device_id=dev, device_id_type=MESH
        )

    def copy_1(t):
        return remote(pay.at[t], buf_1.at[t], 0, r1.at[t], dev_x)

    def copy_2(t):
        return remote(buf_1.at[t], buf_2.at[t], 1, r2.at[t], dev_a)

    def copy_3(t):
        return remote(buf_2.at[t], buf_3.at[t], 2, r3.at[t], dev_b)

    def copy_s(t):
        return remote(fresh.at[t, 0], fresh.at[t, 1], 3, rs.at[t], dev_s)

    def copy_up_one(t, slot):
        return remote(fresh.at[t, slot], fresh.at[t, 6 + slot], 4 + 7 * slot, rz.at[0, t], dev_u)

    def copy_down_one(t, slot):
        return remote(fresh.at[t, slot], fresh.at[t, 2 + slot], 5 + 7 * slot, rz.at[1, t], dev_d)

    def copy_xup(t):
        return remote(fresh.at[t, 0], fresh.at[t, 7], 9, rz.at[0, t], dev_xu)

    def copy_xdown(t):
        return remote(fresh.at[t, 0], fresh.at[t, 3], 10, rz.at[1, t], dev_xd)

    def copy_up(t):
        return remote(fresh.at[t, pl.ds(0, 2)], fresh.at[t, pl.ds(6, 2)], 4, rz.at[0, t], dev_u)

    def copy_down(t):
        return remote(fresh.at[t, pl.ds(0, 2)], fresh.at[t, pl.ds(2, 2)], 5, rz.at[1, t], dev_d)

    def copy_fup(t):
        return remote(fresh.at[t, 6], fresh.at[t, 4], 6, rf.at[0, t], dev_u)

    def copy_fdown(t):
        return remote(fresh.at[t, 3], fresh.at[t, 5], 7, rf.at[1, t], dev_d)

    def shared(t):
        first = C - LATE - 2 * SHARES + 1
        return (t >= first) & (t < C - LATE) & (lax.rem(t + 2 * C - first, 2) == 0)

    def copy_half_up(t):
        here = pl.ds(0, R // 2)
        return remote(fresh.at[t, 6, here], fresh.at[t, 4, here], 13, rf.at[0, t], dev_u)

    def copy_half_down(t):
        here = pl.ds(R // 2, R // 2)
        return remote(fresh.at[t, 2, here], fresh.at[t, 4, here], 14, rf.at[1, t], dev_d)

    def copy_x(t, i):
        slot = (6, 2, 4)[i]
        return remote(fresh.at[t, slot], fresh.at[t, slot + 1], 15 + i, rq.at[i, t], dev_s)

    def copy_c(t):
        return remote(fresh.at[t, pl.ds(0, 8)], fresh.at[t, pl.ds(8, 8)], 8, rd.at[t], dev_c)

    def out_copies(g):
        cols = pl.ds(pl.multiple_of(g * W, W), W)
        span = pl.ds(g * J, J)
        return (
            pltpu.make_async_copy(nm_v.at[span], out_master.at[:, :, cols], out_sem.at[0, g]),
            pltpu.make_async_copy(nmom_v.at[span], out_mom.at[:, :, cols], out_sem.at[1, g]),
        )

    def out_key(g):
        cols = pl.ds(pl.multiple_of(g * W, W), W)
        return pltpu.make_async_copy(keys_v.at[g], out_keys.at[:, cols], out_sem.at[2, g])

    def forward(t):
        copy_up(t).wait_recv()
        copy_fup(t).start()
        copy_down(t).wait_recv()
        copy_fdown(t).start()

    def to_sibling(t):
        copy_fup(t).wait_recv()
        copy_fdown(t).wait_recv()
        copy_c(t).start()

    def tick(t, _):
        for g in range(G):
            @pl.when(t == g * J)
            def _():
                for c in load_mi(g):
                    c.wait()

        @pl.when(t < C)
        def _():
            pay[t, 0] = m_v[t].astype(jnp.bfloat16)
            copy_1(t).start()

        t2 = t - OFF_2

        @pl.when((t2 >= 0) & (t2 < C))
        def _():
            copy_1(t2).wait_recv()
            buf_1[t2] = jnp.where(pick_x, buf_1[t2], pay[t2])
            copy_2(t2).start()

        t3 = t - OFF_3

        @pl.when((t3 >= 0) & (t3 < C))
        def _():
            copy_2(t3).wait_recv()
            buf_2[t3] = jnp.where(pick_a, buf_2[t3], buf_1[t3])
            copy_3(t3).start()

        tu = t - OFF_U

        @pl.when(tu == 0)
        def _():
            for g in range(G):
                load_mom(g).wait()

        @pl.when((tu >= 0) & (tu < C))
        def _():
            copy_3(tu).wait_recv()
            their = jnp.where(pick_b, buf_3[tu], buf_2[tu])
            their_m = their[0].astype(jnp.float32)
            their_i = their[1].astype(jnp.float32)
            own_m = m_v[tu]
            own_i = pay[tu, 1].astype(jnp.float32)
            mean_d = ((own_m - own_i) + (their_m - their_i)) * 0.5
            mean_m = (own_m + their_m) * 0.5
            new_mom = 0.9 * mom_v[tu] + mean_d
            new_m = mean_m - 0.7 * (mean_d + 0.9 * new_mom)
            nmom_v[tu] = new_mom
            nm_v[tu] = new_m
            fresh[tu, 0] = new_m.astype(jnp.bfloat16)
            copy_s(tu).start()
            copy_up_one(tu, 0).start()
            copy_down_one(tu, 0).start()

            @pl.when(tu >= C - LATE)
            def _():
                copy_xup(tu).start()
                copy_xdown(tu).start()

        @pl.when((tu >= 0) & (tu < C) & (lax.rem(tu + C, J) == J - 1))
        def _():
            for c in out_copies(lax.div(tu, J)):
                c.start()

        tz = t - OFF_Z

        @pl.when((tz >= 0) & (tz < C))
        def _():
            copy_s(tz).wait_recv()

            @pl.when((tz < C - LATE) & jnp.logical_not(shared(tz)))
            def _():
                copy_up_one(tz, 1).start()
                copy_down_one(tz, 1).start()

            @pl.when(shared(tz))
            def _():
                copy_up_one(tz, 0).wait_recv()
                copy_half_up(tz).start()
                copy_x(tz, 0).start()
                copy_down_one(tz, 0).wait_recv()
                copy_half_down(tz).start()
                copy_x(tz, 1).start()

        tf = t - OFF_F
        tl = tf + EARLY

        @pl.when((tf >= 0) & (tf < C - LATE) & jnp.logical_not(shared(tf)))
        def _():
            forward(tf)

        @pl.when(shared(tf))
        def _():
            copy_half_up(tf).wait_recv()
            copy_half_down(tf).wait_recv()
            copy_x(tf, 2).start()

        @pl.when((tl >= C - LATE) & (tl < C))
        def _():
            forward(tl)

        td = t - OFF_D
        te = td + EARLY

        @pl.when((td >= 0) & (td < C - LATE) & jnp.logical_not(shared(td)))
        def _():
            to_sibling(td)

        @pl.when(shared(td))
        def _():
            for i in range(3):
                copy_x(td, i).wait_recv()
            copy_c(td).start()

        @pl.when((te >= C - LATE) & (te < C))
        def _():
            to_sibling(te)

        tm = t - OFF_M

        @pl.when((tm >= 0) & (tm < C))
        def _():
            copy_c(tm).wait_recv()

        @pl.when(tm == Q - 1)
        def _():
            load_tok.wait()

        u = tm - (Q - 1)

        @pl.when(u >= 0)
        def _():
            q = lax.div(u, Q)
            k = lax.rem(u, Q)
            per_group = rows // SUB
            g = lax.div(q, per_group)
            part = lax.rem(q, per_group)
            first = (part == 0) & (k == 0)
            left, right = [], []
            for i in range(slots_per_tick):
                slot = k * slots_per_tick + i
                half = lax.div(slot, 8)
                low = lax.rem(slot, 8)
                oz = lax.rem(z + lax.div(low, 2), 4)
                ox = lax.rem(xlo + low, 2)
                oc = lax.rem(core + half, 2)
                owner = oz * 4 + ox * 2 + oc
                left.append(tok_v[:, pl.ds(pl.multiple_of(owner * rows + part * SUB, SUB), SUB)])
                right.append(fresh[pl.ds(q * Q, Q), slot].reshape(SUB, W))
            product = jnp.dot(
                jnp.concatenate(left, axis=1), jnp.concatenate(right, axis=0), preferred_element_type=jnp.float32
            )

            @pl.when(first)
            def _():
                acc[...] = product

            @pl.when(jnp.logical_not(first))
            def _():
                acc[...] += product

            @pl.when((part == per_group - 1) & (k == Q - 1))
            def _():
                keys_v[g] = acc[...].astype(jnp.bfloat16)
                out_key(g).start()

        return 0

    lax.fori_loop(0, OFF_M + C + Q - 1, tick, 0)

    early, last = pl.ds(0, C - LATE - SHARES), pl.ds(C - LATE, LATE)
    plain, some, half = pl.ds(0, C - SHARES), pl.ds(0, SHARES), pl.ds(0, R // 2)
    everything = (
        (pay, buf_1, 0, r1.at[0], dev_x),
        (buf_1, buf_2, 1, r2.at[0], dev_a),
        (buf_2, buf_3, 2, r3.at[0], dev_b),
        (fresh.at[:, 0], fresh.at[:, 1], 3, rs.at[0], dev_s),
        (fresh.at[:, 0], fresh.at[:, 6], 4, rz.at[0, 0], dev_u),
        (fresh.at[:, 0], fresh.at[:, 2], 5, rz.at[1, 0], dev_d),
        (fresh.at[early, 1], fresh.at[early, 7], 11, rz.at[0, 0], dev_u),
        (fresh.at[early, 1], fresh.at[early, 3], 12, rz.at[1, 0], dev_d),
        (fresh.at[last, 0], fresh.at[last, 7], 9, rz.at[0, 0], dev_xu),
        (fresh.at[last, 0], fresh.at[last, 3], 10, rz.at[1, 0], dev_xd),
        (fresh.at[plain, 6], fresh.at[plain, 4], 6, rf.at[0, 0], dev_u),
        (fresh.at[plain, 3], fresh.at[plain, 5], 7, rf.at[1, 0], dev_d),
        (fresh.at[some, 6, half], fresh.at[some, 4, half], 13, rf.at[0, 0], dev_u),
        (fresh.at[some, 2, half], fresh.at[some, 4, half], 14, rf.at[1, 0], dev_d),
        (fresh.at[some, 6], fresh.at[some, 7], 15, rq.at[0, 0], dev_s),
        (fresh.at[some, 2], fresh.at[some, 3], 16, rq.at[1, 0], dev_s),
        (fresh.at[some, 4], fresh.at[some, 5], 17, rq.at[2, 0], dev_s),
        (fresh.at[:, pl.ds(0, 8)], fresh.at[:, pl.ds(8, 8)], 8, rd.at[0], dev_c),
    )
    for src, dst, k, recv, dev in everything:
        remote(src, dst, k, recv, dev).wait_send()
    for g in range(G):
        for c in out_copies(g):
            c.wait()
        out_key(g).wait()


def local(inner_weights, master_weights, momentum, tokens, partner):
    rows, cols = master_weights.shape[1:]
    toks, depth = tokens.shape[1:]
    J, G = rows // R, cols // W
    C = G * J
    bf16, f32 = jnp.bfloat16, jnp.float32
    anyspace = pl.BlockSpec(memory_space=pl.ANY)
    dma = pltpu.SemaphoreType.DMA
    new_master, new_mom, keys = pl.pallas_call(
        kernel,
        out_shape=(
            jax.ShapeDtypeStruct((J, R, cols), f32),
            jax.ShapeDtypeStruct((J, R, cols), f32),
            jax.ShapeDtypeStruct((toks, cols), bf16),
        ),
        in_specs=[pl.BlockSpec(memory_space=pltpu.HBM)] * 5,
        out_specs=(anyspace,) * 3,
        scratch_shapes=[
            pltpu.VMEM((C, R, W), f32),
            pltpu.VMEM((C, R, W), f32),
            pltpu.VMEM((C, 2, R, W), bf16),
            pltpu.VMEM((C, 2, R, W), bf16),
            pltpu.VMEM((C, 2, R, W), bf16),
            pltpu.VMEM((C, 2, R, W), bf16),
            pltpu.VMEM((C, R, W), f32),
            pltpu.VMEM((C, R, W), f32),
            pltpu.VMEM((C, 16, R, W), bf16),
            pltpu.VMEM((toks, depth), bf16),
            pltpu.VMEM((G, toks, W), bf16),
            pltpu.VMEM((toks, W), f32),
            pltpu.SMEM((1, 8), jnp.int32),
            dma,
            dma((4, G)),
            dma((18,)),
            dma((C,)),
            dma((C,)),
            dma((C,)),
            dma((C,)),
            dma((2, C)),
            dma((2, C)),
            dma((3, C)),
            dma((C,)),
            dma((3, G)),
        ],
        compiler_params=pltpu.CompilerParams(
            collective_id=0, has_side_effects=True, vmem_limit_bytes=47104 * 1024
        ),
        cost_estimate=pl.CostEstimate(
            flops=2 * toks * depth * cols, bytes_accessed=18 * 1024 * 1024, transcendentals=0
        ),
        name="gossip_keys",
    )(
        partner,
        inner_weights.reshape(J, R, cols),
        master_weights.reshape(J, R, cols),
        momentum.reshape(J, R, cols),
        tokens[0],
    )
    return (
        new_master.reshape(1, rows, cols),
        new_mom.reshape(1, rows, cols),
        keys[None],
    )


def solution(mesh):
    return jax.shard_map(
        local,
        mesh=mesh,
        in_specs=(
            P("rep", "fsdp", None),
            P("rep", "fsdp", None),
            P("rep", "fsdp", None),
            P("rep", "fsdp", None),
            P("fsdp", None),
        ),
        out_specs=(P("rep", "fsdp", None), P("rep", "fsdp", None), P("rep", "fsdp", None)),
        check_vma=False,
    )
```

```python
import functools

import jax
import jax.numpy as jnp
from jax import lax
from jax.experimental import pallas as pl
from jax.experimental.pallas import tpu as pltpu
from jax.sharding import PartitionSpec as P

MESH = pl.DeviceIdType.MESH
R, W = 64, 256
SUB = 128
OFF_2, OFF_3, OFF_U, OFF_Z, OFF_F, OFF_D, OFF_M = 4, 6, 8, 10, 12, 14, 16
LATE = 2
SHARES = 4
EARLY = OFF_Z - OFF_U


def kernel(
    part_ref, inner_ref, master_ref, mom_ref, tok_ref,
    out_master, out_mom, out_keys,
    m_v, mom_v, pay, buf_1, buf_2, buf_3, nm_v, nmom_v, fresh, tok_v, keys_v, acc,
    part_s, part_sem, load_sem, send_sem, r1, r2, r3, rs, rz, rf, rq, rd, out_sem,
):
    J = master_ref.shape[0]
    G = master_ref.shape[2] // W
    C = G * J
    Q = SUB // R
    slots_per_tick = 16 // Q
    rows = J * R

    rep = lax.axis_index("rep")
    fs = lax.axis_index("fsdp")
    rep1 = rep + 1 - 2 * lax.rem(rep, 2)
    rep3 = rep + 3 - 2 * lax.rem(rep, 4)
    rep4 = lax.rem(rep + 4, 8)
    core = lax.rem(fs, 2)
    xlo = lax.rem(lax.div(fs, 2), 2)
    z = lax.div(fs, 4)
    sib = fs + 1 - 2 * core
    xn = fs + 2 - 4 * xlo
    zu = lax.rem(fs + 4, 16)
    zd = lax.rem(fs + 12, 16)

    dev_x, dev_a, dev_b = (rep4, fs), (rep1, fs), (rep3, fs)
    dev_s, dev_u, dev_d, dev_c = (rep, xn), (rep, zu), (rep, zd), (rep, sib)
    dev_xu, dev_xd = (rep, lax.rem(xn + 4, 16)), (rep, lax.rem(xn + 12, 16))

    def load_mi(g):
        cols = pl.ds(g * W, W)
        return (
            pltpu.make_async_copy(master_ref.at[:, :, cols], m_v.at[pl.ds(g * J, J)], load_sem.at[0, g]),
            pltpu.make_async_copy(inner_ref.at[:, :, cols], pay.at[pl.ds(g * J, J), 1], load_sem.at[1, g]),
        )

    def load_mom(g):
        return pltpu.make_async_copy(mom_ref.at[:, :, pl.ds(g * W, W)], mom_v.at[pl.ds(g * J, J)], load_sem.at[2, g])

    load_tok = pltpu.make_async_copy(tok_ref, tok_v, load_sem.at[3, 0])
    for c in load_mi(0):
        c.start()

    load_part = pltpu.make_async_copy(part_ref, part_s, part_sem)
    load_part.start()
    barrier = pltpu.get_barrier_semaphore()
    for d in (dev_a, dev_b, dev_x, dev_s, dev_u, dev_d, dev_c, dev_xu, dev_xd):
        pl.semaphore_signal(barrier, inc=1, device_id=d, device_id_type=MESH)
    pl.semaphore_wait(barrier, 9)
    for g in range(1, G):
        for c in load_mi(g):
            c.start()
    for g in range(G):
        load_mom(g).start()
    load_tok.start()

    load_part.wait()
    mask = jnp.bitwise_xor(part_s[0, rep], rep)
    bit1 = lax.rem(lax.div(mask, 2), 2)
    pick_a = lax.rem(lax.rem(mask, 2) + bit1, 2) == 1
    pick_b = bit1 == 1
    pick_x = lax.div(mask, 4) == 1

    def remote(src, dst, k, recv, dev):
        return pltpu.make_async_remote_copy(
            src_ref=src, dst_ref=dst, send_sem=send_sem.at[k], recv_sem=recv, device_id=dev, device_id_type=MESH
        )

    def copy_1(t):
        return remote(pay.at[t], buf_1.at[t], 0, r1.at[t], dev_x)

    def copy_2(t):
        return remote(buf_1.at[t], buf_2.at[t], 1, r2.at[t], dev_a)

    def copy_3(t):
        return remote(buf_2.at[t], buf_3.at[t], 2, r3.at[t], dev_b)

    def copy_s(t):
        return remote(fresh.at[t, 0], fresh.at[t, 1], 3, rs.at[t], dev_s)

    def copy_up_one(t, slot):
        return remote(fresh.at[t, slot], fresh.at[t, 6 + slot], 4 + 7 * slot, rz.at[0, t], dev_u)

    def copy_down_one(t, slot):
        return remote(fresh.at[t, slot], fresh.at[t, 2 + slot], 5 + 7 * slot, rz.at[1, t], dev_d)

    def copy_xup(t):
        return remote(fresh.at[t, 0], fresh.at[t, 7], 9, rz.at[0, t], dev_xu)

    def copy_xdown(t):
        return remote(fresh.at[t, 0], fresh.at[t, 3], 10, rz.at[1, t], dev_xd)

    def copy_up(t):
        return remote(fresh.at[t, pl.ds(0, 2)], fresh.at[t, pl.ds(6, 2)], 4, rz.at[0, t], dev_u)

    def copy_down(t):
        return remote(fresh.at[t, pl.ds(0, 2)], fresh.at[t, pl.ds(2, 2)], 5, rz.at[1, t], dev_d)

    def copy_fup(t):
        return remote(fresh.at[t, 6], fresh.at[t, 4], 6, rf.at[0, t], dev_u)

    def copy_fdown(t):
        return remote(fresh.at[t, 3], fresh.at[t, 5], 7, rf.at[1, t], dev_d)

    def shared(t):
        first = C - LATE - 2 * SHARES + 1
        return (t >= first) & (t < C - LATE) & (lax.rem(t + 2 * C - first, 2) == 0)

    def copy_half_up(t):
        here = pl.ds(0, R // 2)
        return remote(fresh.at[t, 6, here], fresh.at[t, 4, here], 13, rf.at[0, t], dev_u)

    def copy_half_down(t):
        here = pl.ds(R // 2, R // 2)
        return remote(fresh.at[t, 2, here], fresh.at[t, 4, here], 14, rf.at[1, t], dev_d)

    def copy_x(t, i):
        slot = (6, 2, 4)[i]
        return remote(fresh.at[t, slot], fresh.at[t, slot + 1], 15 + i, rq.at[i, t], dev_s)

    def copy_c(t):
        return remote(fresh.at[t, pl.ds(0, 8)], fresh.at[t, pl.ds(8, 8)], 8, rd.at[t], dev_c)

    def out_copies(g):
        cols = pl.ds(pl.multiple_of(g * W, W), W)
        span = pl.ds(g * J, J)
        return (
            pltpu.make_async_copy(nm_v.at[span], out_master.at[:, :, cols], out_sem.at[0, g]),
            pltpu.make_async_copy(nmom_v.at[span], out_mom.at[:, :, cols], out_sem.at[1, g]),
        )

    def out_key(g):
        cols = pl.ds(pl.multiple_of(g * W, W), W)
        return pltpu.make_async_copy(keys_v.at[g], out_keys.at[:, cols], out_sem.at[2, g])

    def forward(t):
        copy_up(t).wait_recv()
        copy_fup(t).start()
        copy_down(t).wait_recv()
        copy_fdown(t).start()

    def to_sibling(t):
        copy_fup(t).wait_recv()
        copy_fdown(t).wait_recv()
        copy_c(t).start()

    def tick(t, _):
        for g in range(G):
            @pl.when(t == g * J)
            def _():
                for c in load_mi(g):
                    c.wait()

        @pl.when(t < C)
        def _():
            pay[t, 0] = m_v[t].astype(jnp.bfloat16)
            copy_1(t).start()

        t2 = t - OFF_2

        @pl.when((t2 >= 0) & (t2 < C))
        def _():
            copy_1(t2).wait_recv()
            buf_1[t2] = jnp.where(pick_x, buf_1[t2], pay[t2])
            copy_2(t2).start()

        t3 = t - OFF_3

        @pl.when((t3 >= 0) & (t3 < C))
        def _():
            copy_2(t3).wait_recv()
            buf_2[t3] = jnp.where(pick_a, buf_2[t3], buf_1[t3])
            copy_3(t3).start()

        tu = t - OFF_U

        @pl.when(tu == 0)
        def _():
            for g in range(G):
                load_mom(g).wait()

        @pl.when((tu >= 0) & (tu < C))
        def _():
            copy_3(tu).wait_recv()
            their = jnp.where(pick_b, buf_3[tu], buf_2[tu])
            their_m = their[0].astype(jnp.float32)
            their_i = their[1].astype(jnp.float32)
            own_m = m_v[tu]
            own_i = pay[tu, 1].astype(jnp.float32)
            mean_d = ((own_m - own_i) + (their_m - their_i)) * 0.5
            mean_m = (own_m + their_m) * 0.5
            new_mom = 0.9 * mom_v[tu] + mean_d
            new_m = mean_m - 0.7 * (mean_d + 0.9 * new_mom)
            nmom_v[tu] = new_mom
            nm_v[tu] = new_m
            fresh[tu, 0] = new_m.astype(jnp.bfloat16)
            copy_s(tu).start()
            copy_up_one(tu, 0).start()
            copy_down_one(tu, 0).start()

            @pl.when(tu >= C - LATE)
            def _():
                copy_xup(tu).start()
                copy_xdown(tu).start()

        @pl.when((tu >= 0) & (tu < C) & (lax.rem(tu + C, J) == J - 1))
        def _():
            for c in out_copies(lax.div(tu, J)):
                c.start()

        tz = t - OFF_Z

        @pl.when((tz >= 0) & (tz < C))
        def _():
            copy_s(tz).wait_recv()

            @pl.when((tz < C - LATE) & jnp.logical_not(shared(tz)))
            def _():
                copy_up_one(tz, 1).start()
                copy_down_one(tz, 1).start()

            @pl.when(shared(tz))
            def _():
                copy_up_one(tz, 0).wait_recv()
                copy_half_up(tz).start()
                copy_x(tz, 0).start()
                copy_down_one(tz, 0).wait_recv()
                copy_half_down(tz).start()
                copy_x(tz, 1).start()

        tf = t - OFF_F
        tl = tf + EARLY

        @pl.when((tf >= 0) & (tf < C - LATE) & jnp.logical_not(shared(tf)))
        def _():
            forward(tf)

        @pl.when(shared(tf))
        def _():
            copy_half_up(tf).wait_recv()
            copy_half_down(tf).wait_recv()
            copy_x(tf, 2).start()

        @pl.when((tl >= C - LATE) & (tl < C))
        def _():
            forward(tl)

        tm = t - OFF_M

        @pl.when((tm >= 0) & (tm < C))
        def _():
            copy_c(tm).wait_recv()

        @pl.when(tm == Q - 1)
        def _():
            load_tok.wait()

        u = tm - (Q - 1)

        @pl.when(u >= 0)
        def _():
            q = lax.div(u, Q)
            k = lax.rem(u, Q)
            per_group = rows // SUB
            g = lax.div(q, per_group)
            part = lax.rem(q, per_group)
            first = (part == 0) & (k == 0)
            left, right = [], []
            for i in range(slots_per_tick):
                slot = k * slots_per_tick + i
                half = lax.div(slot, 8)
                low = lax.rem(slot, 8)
                oz = lax.rem(z + lax.div(low, 2), 4)
                ox = lax.rem(xlo + low, 2)
                oc = lax.rem(core + half, 2)
                owner = oz * 4 + ox * 2 + oc
                left.append(tok_v[:, pl.ds(pl.multiple_of(owner * rows + part * SUB, SUB), SUB)])
                right.append(fresh[pl.ds(q * Q, Q), slot].reshape(SUB, W))
            product = jnp.dot(
                jnp.concatenate(left, axis=1), jnp.concatenate(right, axis=0), preferred_element_type=jnp.float32
            )

            @pl.when(first)
            def _():
                acc[...] = product

            @pl.when(jnp.logical_not(first))
            def _():
                acc[...] += product

            @pl.when((part == per_group - 1) & (k == Q - 1))
            def _():
                keys_v[g] = acc[...].astype(jnp.bfloat16)
                out_key(g).start()

        td = t - OFF_D
        te = td + EARLY

        @pl.when((td >= 0) & (td < C - LATE) & jnp.logical_not(shared(td)))
        def _():
            to_sibling(td)

        @pl.when(shared(td))
        def _():
            for i in range(3):
                copy_x(td, i).wait_recv()
            copy_c(td).start()

        @pl.when((te >= C - LATE) & (te < C))
        def _():
            to_sibling(te)

        return 0

    lax.fori_loop(0, OFF_M + C + Q - 1, tick, 0)

    early, last = pl.ds(0, C - LATE - SHARES), pl.ds(C - LATE, LATE)
    plain, some, half = pl.ds(0, C - SHARES), pl.ds(0, SHARES), pl.ds(0, R // 2)
    everything = (
        (pay, buf_1, 0, r1.at[0], dev_x),
        (buf_1, buf_2, 1, r2.at[0], dev_a),
        (buf_2, buf_3, 2, r3.at[0], dev_b),
        (fresh.at[:, 0], fresh.at[:, 1], 3, rs.at[0], dev_s),
        (fresh.at[:, 0], fresh.at[:, 6], 4, rz.at[0, 0], dev_u),
        (fresh.at[:, 0], fresh.at[:, 2], 5, rz.at[1, 0], dev_d),
        (fresh.at[early, 1], fresh.at[early, 7], 11, rz.at[0, 0], dev_u),
        (fresh.at[early, 1], fresh.at[early, 3], 12, rz.at[1, 0], dev_d),
        (fresh.at[last, 0], fresh.at[last, 7], 9, rz.at[0, 0], dev_xu),
        (fresh.at[last, 0], fresh.at[last, 3], 10, rz.at[1, 0], dev_xd),
        (fresh.at[plain, 6], fresh.at[plain, 4], 6, rf.at[0, 0], dev_u),
        (fresh.at[plain, 3], fresh.at[plain, 5], 7, rf.at[1, 0], dev_d),
        (fresh.at[some, 6, half], fresh.at[some, 4, half], 13, rf.at[0, 0], dev_u),
        (fresh.at[some, 2, half], fresh.at[some, 4, half], 14, rf.at[1, 0], dev_d),
        (fresh.at[some, 6], fresh.at[some, 7], 15, rq.at[0, 0], dev_s),
        (fresh.at[some, 2], fresh.at[some, 3], 16, rq.at[1, 0], dev_s),
        (fresh.at[some, 4], fresh.at[some, 5], 17, rq.at[2, 0], dev_s),
        (fresh.at[:, pl.ds(0, 8)], fresh.at[:, pl.ds(8, 8)], 8, rd.at[0], dev_c),
    )
    for src, dst, k, recv, dev in everything:
        remote(src, dst, k, recv, dev).wait_send()
    for g in range(G):
        for c in out_copies(g):
            c.wait()
        out_key(g).wait()


def local(inner_weights, master_weights, momentum, tokens, partner):
    rows, cols = master_weights.shape[1:]
    toks, depth = tokens.shape[1:]
    J, G = rows // R, cols // W
    C = G * J
    bf16, f32 = jnp.bfloat16, jnp.float32
    anyspace = pl.BlockSpec(memory_space=pl.ANY)
    dma = pltpu.SemaphoreType.DMA
    new_master, new_mom, keys = pl.pallas_call(
        kernel,
        out_shape=(
            jax.ShapeDtypeStruct((J, R, cols), f32),
            jax.ShapeDtypeStruct((J, R, cols), f32),
            jax.ShapeDtypeStruct((toks, cols), bf16),
        ),
        in_specs=[pl.BlockSpec(memory_space=pltpu.HBM)] * 5,
        out_specs=(anyspace,) * 3,
        scratch_shapes=[
            pltpu.VMEM((C, R, W), f32),
            pltpu.VMEM((C, R, W), f32),
            pltpu.VMEM((C, 2, R, W), bf16),
            pltpu.VMEM((C, 2, R, W), bf16),
            pltpu.VMEM((C, 2, R, W), bf16),
            pltpu.VMEM((C, 2, R, W), bf16),
            pltpu.VMEM((C, R, W), f32),
            pltpu.VMEM((C, R, W), f32),
            pltpu.VMEM((C, 16, R, W), bf16),
            pltpu.VMEM((toks, depth), bf16),
            pltpu.VMEM((G, toks, W), bf16),
            pltpu.VMEM((toks, W), f32),
            pltpu.SMEM((1, 8), jnp.int32),
            dma,
            dma((4, G)),
            dma((18,)),
            dma((C,)),
            dma((C,)),
            dma((C,)),
            dma((C,)),
            dma((2, C)),
            dma((2, C)),
            dma((3, C)),
            dma((C,)),
            dma((3, G)),
        ],
        compiler_params=pltpu.CompilerParams(
            collective_id=0, has_side_effects=True, vmem_limit_bytes=47104 * 1024
        ),
        cost_estimate=pl.CostEstimate(
            flops=2 * toks * depth * cols, bytes_accessed=18 * 1024 * 1024, transcendentals=0
        ),
        name="gossip_keys",
    )(
        partner,
        inner_weights.reshape(J, R, cols),
        master_weights.reshape(J, R, cols),
        momentum.reshape(J, R, cols),
        tokens[0],
    )
    return (
        new_master.reshape(1, rows, cols),
        new_mom.reshape(1, rows, cols),
        keys[None],
    )


def solution(mesh):
    return jax.shard_map(
        local,
        mesh=mesh,
        in_specs=(
            P("rep", "fsdp", None),
            P("rep", "fsdp", None),
            P("rep", "fsdp", None),
            P("rep", "fsdp", None),
            P("fsdp", None),
        ),
        out_specs=(P("rep", "fsdp", None), P("rep", "fsdp", None), P("rep", "fsdp", None)),
        check_vma=False,
    )
```

```python
import functools

import jax
import jax.numpy as jnp
from jax import lax
from jax.experimental import pallas as pl
from jax.experimental.pallas import tpu as pltpu
from jax.sharding import PartitionSpec as P

MESH = pl.DeviceIdType.MESH
R, W = 64, 256
SUB = 128
OFF_2, OFF_3, OFF_U, OFF_Z, OFF_F, OFF_D, OFF_M = 3, 5, 7, 9, 11, 13, 15
LATE = 2
SHARES = 3
EARLY = OFF_Z - OFF_U


def kernel(
    part_ref, inner_ref, master_ref, mom_ref, tok_ref,
    out_master, out_mom, out_keys,
    m_v, mom_v, pay, buf_1, buf_2, buf_3, nm_v, nmom_v, fresh, tok_v, keys_v, acc,
    part_s, part_sem, load_sem, send_sem, r1, r2, r3, rs, rz, rf, rq, rd, out_sem,
):
    J = master_ref.shape[0]
    G = master_ref.shape[2] // W
    C = G * J
    Q = SUB // R
    slots_per_tick = 16 // Q
    rows = J * R

    rep = lax.axis_index("rep")
    fs = lax.axis_index("fsdp")
    rep1 = rep + 1 - 2 * lax.rem(rep, 2)
    rep3 = rep + 3 - 2 * lax.rem(rep, 4)
    rep4 = lax.rem(rep + 4, 8)
    core = lax.rem(fs, 2)
    xlo = lax.rem(lax.div(fs, 2), 2)
    z = lax.div(fs, 4)
    sib = fs + 1 - 2 * core
    xn = fs + 2 - 4 * xlo
    zu = lax.rem(fs + 4, 16)
    zd = lax.rem(fs + 12, 16)

    dev_x, dev_a, dev_b = (rep4, fs), (rep1, fs), (rep3, fs)
    dev_s, dev_u, dev_d, dev_c = (rep, xn), (rep, zu), (rep, zd), (rep, sib)
    dev_xu, dev_xd = (rep, lax.rem(xn + 4, 16)), (rep, lax.rem(xn + 12, 16))

    def load_mi(g):
        cols = pl.ds(g * W, W)
        return (
            pltpu.make_async_copy(master_ref.at[:, :, cols], m_v.at[pl.ds(g * J, J)], load_sem.at[0, g]),
            pltpu.make_async_copy(inner_ref.at[:, :, cols], pay.at[pl.ds(g * J, J), 1], load_sem.at[1, g]),
        )

    def load_mom(g):
        return pltpu.make_async_copy(mom_ref.at[:, :, pl.ds(g * W, W)], mom_v.at[pl.ds(g * J, J)], load_sem.at[2, g])

    load_tok = pltpu.make_async_copy(tok_ref, tok_v, load_sem.at[3, 0])
    for c in load_mi(0):
        c.start()

    load_part = pltpu.make_async_copy(part_ref, part_s, part_sem)
    load_part.start()
    barrier = pltpu.get_barrier_semaphore()
    for d in (dev_a, dev_b, dev_x, dev_s, dev_u, dev_d, dev_c, dev_xu, dev_xd):
        pl.semaphore_signal(barrier, inc=1, device_id=d, device_id_type=MESH)
    pl.semaphore_wait(barrier, 9)
    for g in range(1, G):
        for c in load_mi(g):
            c.start()
    for g in range(G):
        load_mom(g).start()
    load_tok.start()

    load_part.wait()
    mask = jnp.bitwise_xor(part_s[0, rep], rep)
    bit1 = lax.rem(lax.div(mask, 2), 2)
    pick_a = lax.rem(lax.rem(mask, 2) + bit1, 2) == 1
    pick_b = bit1 == 1
    pick_x = lax.div(mask, 4) == 1

    def remote(src, dst, k, recv, dev):
        return pltpu.make_async_remote_copy(
            src_ref=src, dst_ref=dst, send_sem=send_sem.at[k], recv_sem=recv, device_id=dev, device_id_type=MESH
        )

    def copy_1(t):
        return remote(pay.at[t], buf_1.at[t], 0, r1.at[t], dev_x)

    def copy_2(t):
        return remote(buf_1.at[t], buf_2.at[t], 1, r2.at[t], dev_a)

    def copy_3(t):
        return remote(buf_2.at[t], buf_3.at[t], 2, r3.at[t], dev_b)

    def copy_s(t):
        return remote(fresh.at[t, 0], fresh.at[t, 1], 3, rs.at[t], dev_s)

    def copy_up_one(t, slot):
        return remote(fresh.at[t, slot], fresh.at[t, 6 + slot], 4 + 7 * slot, rz.at[0, t], dev_u)

    def copy_down_one(t, slot):
        return remote(fresh.at[t, slot], fresh.at[t, 2 + slot], 5 + 7 * slot, rz.at[1, t], dev_d)

    def copy_xup(t):
        return remote(fresh.at[t, 0], fresh.at[t, 7], 9, rz.at[0, t], dev_xu)

    def copy_xdown(t):
        return remote(fresh.at[t, 0], fresh.at[t, 3], 10, rz.at[1, t], dev_xd)

    def copy_up(t):
        return remote(fresh.at[t, pl.ds(0, 2)], fresh.at[t, pl.ds(6, 2)], 4, rz.at[0, t], dev_u)

    def copy_down(t):
        return remote(fresh.at[t, pl.ds(0, 2)], fresh.at[t, pl.ds(2, 2)], 5, rz.at[1, t], dev_d)

    def copy_fup(t):
        return remote(fresh.at[t, 6], fresh.at[t, 4], 6, rf.at[0, t], dev_u)

    def copy_fdown(t):
        return remote(fresh.at[t, 3], fresh.at[t, 5], 7, rf.at[1, t], dev_d)

    def shared(t):
        first = C - LATE - 2 * SHARES + 1
        return (t >= first) & (t < C - LATE) & (lax.rem(t + 2 * C - first, 2) == 0)

    def copy_half_up(t):
        here = pl.ds(0, R // 2)
        return remote(fresh.at[t, 6, here], fresh.at[t, 4, here], 13, rf.at[0, t], dev_u)

    def copy_half_down(t):
        here = pl.ds(R // 2, R // 2)
        return remote(fresh.at[t, 2, here], fresh.at[t, 4, here], 14, rf.at[1, t], dev_d)

    def copy_x(t, i):
        slot = (6, 2, 4)[i]
        return remote(fresh.at[t, slot], fresh.at[t, slot + 1], 15 + i, rq.at[i, t], dev_s)

    def copy_c(t):
        return remote(fresh.at[t, pl.ds(0, 8)], fresh.at[t, pl.ds(8, 8)], 8, rd.at[t], dev_c)

    def out_copies(g):
        cols = pl.ds(pl.multiple_of(g * W, W), W)
        span = pl.ds(g * J, J)
        return (
            pltpu.make_async_copy(nm_v.at[span], out_master.at[:, :, cols], out_sem.at[0, g]),
            pltpu.make_async_copy(nmom_v.at[span], out_mom.at[:, :, cols], out_sem.at[1, g]),
        )

    def out_key(g):
        cols = pl.ds(pl.multiple_of(g * W, W), W)
        return pltpu.make_async_copy(keys_v.at[g], out_keys.at[:, cols], out_sem.at[2, g])

    def forward(t):
        copy_up(t).wait_recv()
        copy_fup(t).start()
        copy_down(t).wait_recv()
        copy_fdown(t).start()

    def to_sibling(t):
        copy_fup(t).wait_recv()
        copy_fdown(t).wait_recv()
        copy_c(t).start()

    def tick(t, _):
        for g in range(G):
            @pl.when(t == g * J)
            def _():
                for c in load_mi(g):
                    c.wait()

        @pl.when(t < C)
        def _():
            pay[t, 0] = m_v[t].astype(jnp.bfloat16)
            copy_1(t).start()

        t2 = t - OFF_2

        @pl.when((t2 >= 0) & (t2 < C))
        def _():
            copy_1(t2).wait_recv()
            buf_1[t2] = jnp.where(pick_x, buf_1[t2], pay[t2])
            copy_2(t2).start()

        t3 = t - OFF_3

        @pl.when((t3 >= 0) & (t3 < C))
        def _():
            copy_2(t3).wait_recv()
            buf_2[t3] = jnp.where(pick_a, buf_2[t3], buf_1[t3])
            copy_3(t3).start()

        tu = t - OFF_U

        @pl.when(tu == 0)
        def _():
            for g in range(G):
                load_mom(g).wait()

        @pl.when((tu >= 0) & (tu < C))
        def _():
            copy_3(tu).wait_recv()
            their = jnp.where(pick_b, buf_3[tu], buf_2[tu])
            their_m = their[0].astype(jnp.float32)
            their_i = their[1].astype(jnp.float32)
            own_m = m_v[tu]
            own_i = pay[tu, 1].astype(jnp.float32)
            mean_d = ((own_m - own_i) + (their_m - their_i)) * 0.5
            mean_m = (own_m + their_m) * 0.5
            new_mom = 0.9 * mom_v[tu] + mean_d
            new_m = mean_m - 0.7 * (mean_d + 0.9 * new_mom)
            nmom_v[tu] = new_mom
            nm_v[tu] = new_m
            fresh[tu, 0] = new_m.astype(jnp.bfloat16)
            copy_s(tu).start()
            copy_up_one(tu, 0).start()
            copy_down_one(tu, 0).start()

            @pl.when(tu >= C - LATE)
            def _():
                copy_xup(tu).start()
                copy_xdown(tu).start()

        @pl.when((tu >= 0) & (tu < C) & (lax.rem(tu + C, J) == J - 1))
        def _():
            for c in out_copies(lax.div(tu, J)):
                c.start()

        tz = t - OFF_Z

        @pl.when((tz >= 0) & (tz < C))
        def _():
            copy_s(tz).wait_recv()

            @pl.when((tz < C - LATE) & jnp.logical_not(shared(tz)))
            def _():
                copy_up_one(tz, 1).start()
                copy_down_one(tz, 1).start()

            @pl.when(shared(tz))
            def _():
                copy_up_one(tz, 0).wait_recv()
                copy_half_up(tz).start()
                copy_x(tz, 0).start()
                copy_down_one(tz, 0).wait_recv()
                copy_half_down(tz).start()
                copy_x(tz, 1).start()

        tf = t - OFF_F
        tl = tf + EARLY

        @pl.when((tf >= 0) & (tf < C - LATE) & jnp.logical_not(shared(tf)))
        def _():
            forward(tf)

        @pl.when(shared(tf))
        def _():
            copy_half_up(tf).wait_recv()
            copy_half_down(tf).wait_recv()
            copy_x(tf, 2).start()

        @pl.when((tl >= C - LATE) & (tl < C))
        def _():
            forward(tl)

        tm = t - OFF_M

        @pl.when((tm >= 0) & (tm < C))
        def _():
            copy_c(tm).wait_recv()

        @pl.when(tm == Q - 1)
        def _():
            load_tok.wait()

        u = tm - (Q - 1)

        @pl.when(u >= 0)
        def _():
            q = lax.div(u, Q)
            k = lax.rem(u, Q)
            per_group = rows // SUB
            g = lax.div(q, per_group)
            part = lax.rem(q, per_group)
            first = (part == 0) & (k == 0)
            left, right = [], []
            for i in range(slots_per_tick):
                slot = k * slots_per_tick + i
                half = lax.div(slot, 8)
                low = lax.rem(slot, 8)
                oz = lax.rem(z + lax.div(low, 2), 4)
                ox = lax.rem(xlo + low, 2)
                oc = lax.rem(core + half, 2)
                owner = oz * 4 + ox * 2 + oc
                left.append(tok_v[:, pl.ds(pl.multiple_of(owner * rows + part * SUB, SUB), SUB)])
                right.append(fresh[pl.ds(q * Q, Q), slot].reshape(SUB, W))
            product = jnp.dot(
                jnp.concatenate(left, axis=1), jnp.concatenate(right, axis=0), preferred_element_type=jnp.float32
            )

            @pl.when(first)
            def _():
                acc[...] = product

            @pl.when(jnp.logical_not(first))
            def _():
                acc[...] += product

            @pl.when((part == per_group - 1) & (k == Q - 1))
            def _():
                keys_v[g] = acc[...].astype(jnp.bfloat16)
                out_key(g).start()

        td = t - OFF_D
        te = td + EARLY

        @pl.when((td >= 0) & (td < C - LATE) & jnp.logical_not(shared(td)))
        def _():
            to_sibling(td)

        @pl.when(shared(td))
        def _():
            for i in range(3):
                copy_x(td, i).wait_recv()
            copy_c(td).start()

        @pl.when((te >= C - LATE) & (te < C))
        def _():
            to_sibling(te)

        return 0

    lax.fori_loop(0, OFF_M + C + Q - 1, tick, 0)

    early, last = pl.ds(0, C - LATE - SHARES), pl.ds(C - LATE, LATE)
    plain, some, half = pl.ds(0, C - SHARES), pl.ds(0, SHARES), pl.ds(0, R // 2)
    everything = (
        (pay, buf_1, 0, r1.at[0], dev_x),
        (buf_1, buf_2, 1, r2.at[0], dev_a),
        (buf_2, buf_3, 2, r3.at[0], dev_b),
        (fresh.at[:, 0], fresh.at[:, 1], 3, rs.at[0], dev_s),
        (fresh.at[:, 0], fresh.at[:, 6], 4, rz.at[0, 0], dev_u),
        (fresh.at[:, 0], fresh.at[:, 2], 5, rz.at[1, 0], dev_d),
        (fresh.at[early, 1], fresh.at[early, 7], 11, rz.at[0, 0], dev_u),
        (fresh.at[early, 1], fresh.at[early, 3], 12, rz.at[1, 0], dev_d),
        (fresh.at[last, 0], fresh.at[last, 7], 9, rz.at[0, 0], dev_xu),
        (fresh.at[last, 0], fresh.at[last, 3], 10, rz.at[1, 0], dev_xd),
        (fresh.at[plain, 6], fresh.at[plain, 4], 6, rf.at[0, 0], dev_u),
        (fresh.at[plain, 3], fresh.at[plain, 5], 7, rf.at[1, 0], dev_d),
        (fresh.at[some, 6, half], fresh.at[some, 4, half], 13, rf.at[0, 0], dev_u),
        (fresh.at[some, 2, half], fresh.at[some, 4, half], 14, rf.at[1, 0], dev_d),
        (fresh.at[some, 6], fresh.at[some, 7], 15, rq.at[0, 0], dev_s),
        (fresh.at[some, 2], fresh.at[some, 3], 16, rq.at[1, 0], dev_s),
        (fresh.at[some, 4], fresh.at[some, 5], 17, rq.at[2, 0], dev_s),
        (fresh.at[:, pl.ds(0, 8)], fresh.at[:, pl.ds(8, 8)], 8, rd.at[0], dev_c),
    )
    for src, dst, k, recv, dev in everything:
        remote(src, dst, k, recv, dev).wait_send()
    for g in range(G):
        for c in out_copies(g):
            c.wait()
        out_key(g).wait()


def local(inner_weights, master_weights, momentum, tokens, partner):
    rows, cols = master_weights.shape[1:]
    toks, depth = tokens.shape[1:]
    J, G = rows // R, cols // W
    C = G * J
    bf16, f32 = jnp.bfloat16, jnp.float32
    anyspace = pl.BlockSpec(memory_space=pl.ANY)
    dma = pltpu.SemaphoreType.DMA
    new_master, new_mom, keys = pl.pallas_call(
        kernel,
        out_shape=(
            jax.ShapeDtypeStruct((J, R, cols), f32),
            jax.ShapeDtypeStruct((J, R, cols), f32),
            jax.ShapeDtypeStruct((toks, cols), bf16),
        ),
        in_specs=[pl.BlockSpec(memory_space=pltpu.HBM)] * 5,
        out_specs=(anyspace,) * 3,
        scratch_shapes=[
            pltpu.VMEM((C, R, W), f32),
            pltpu.VMEM((C, R, W), f32),
            pltpu.VMEM((C, 2, R, W), bf16),
            pltpu.VMEM((C, 2, R, W), bf16),
            pltpu.VMEM((C, 2, R, W), bf16),
            pltpu.VMEM((C, 2, R, W), bf16),
            pltpu.VMEM((C, R, W), f32),
            pltpu.VMEM((C, R, W), f32),
            pltpu.VMEM((C, 16, R, W), bf16),
            pltpu.VMEM((toks, depth), bf16),
            pltpu.VMEM((G, toks, W), bf16),
            pltpu.VMEM((toks, W), f32),
            pltpu.SMEM((1, 8), jnp.int32),
            dma,
            dma((4, G)),
            dma((18,)),
            dma((C,)),
            dma((C,)),
            dma((C,)),
            dma((C,)),
            dma((2, C)),
            dma((2, C)),
            dma((3, C)),
            dma((C,)),
            dma((3, G)),
        ],
        compiler_params=pltpu.CompilerParams(
            collective_id=0, has_side_effects=True, vmem_limit_bytes=47104 * 1024
        ),
        cost_estimate=pl.CostEstimate(
            flops=2 * toks * depth * cols, bytes_accessed=18 * 1024 * 1024, transcendentals=0
        ),
        name="gossip_keys",
    )(
        partner,
        inner_weights.reshape(J, R, cols),
        master_weights.reshape(J, R, cols),
        momentum.reshape(J, R, cols),
        tokens[0],
    )
    return (
        new_master.reshape(1, rows, cols),
        new_mom.reshape(1, rows, cols),
        keys[None],
    )


def solution(mesh):
    return jax.shard_map(
        local,
        mesh=mesh,
        in_specs=(
            P("rep", "fsdp", None),
            P("rep", "fsdp", None),
            P("rep", "fsdp", None),
            P("rep", "fsdp", None),
            P("fsdp", None),
        ),
        out_specs=(P("rep", "fsdp", None), P("rep", "fsdp", None), P("rep", "fsdp", None)),
        check_vma=False,
    )
```
